32 devices in a mesh: dp: 16 (over z, y, x), tensor: 2 (over core).
Axes of the slice: x: 2, y: 2, z: 4, core: 2. Of those that a mesh axis runs over, the one named last changes fastest.
Arguments:
- tokens: bfloat16 [8192, 1024], P(('dp', 'tensor')), may hold values from -12 to 12
- enc_states: bfloat16 [4096, 1024], P(('dp', 'tensor')), may hold values from -12 to 12
- utt_lengths: int32 [16], P('dp'), may hold values from 256 to 512, as said below
- enc_lengths: int32 [16], P('dp'), may hold values from 128 to 256, as said below
- self_qkv: bfloat16 [3, 1024, 1024], P(None, 'dp', 'tensor'), may hold values from -0.1875 to 0.1875
- self_out: bfloat16 [1024, 1024], P('dp', 'tensor'), may hold values from -2 to 2
- cross_qkv: bfloat16 [3, 1024, 1024], P(None, 'dp', 'tensor'), may hold values from -0.1875 to 0.1875
- cross_out: bfloat16 [1024, 1024], P('dp', 'tensor'), may hold values from -1.5 to 1.5
- ffn_proj: bfloat16 [2, 1024, 4096], P(None, 'dp', 'tensor'), may hold values from -0.1875 to 0.1875
- norm_gains: bfloat16 [4, 1024], P(None, 'dp'), may hold values from 0.25 to 1.75
- norm_biases: bfloat16 [4, 1024], P(None, 'dp'), may hold values from -1.25 to 1.25
- cotangent: bfloat16 [8192, 1024], P(('dp', 'tensor')), may hold values from -12 to 12
Outputs:
- output: bfloat16 [8192, 1024], P(('dp', 'tensor'))
- token_grad: float32 [8192, 1024], P(('dp', 'tensor'))
- enc_grad: float32 [4096, 1024], P(('dp', 'tensor'))
- self_qkv_grad: float32 [3, 1024, 1024], P(None, 'dp', 'tensor')
- self_out_grad: float32 [1024, 1024], P('dp', 'tensor')
- cross_qkv_grad: float32 [3, 1024, 1024], P(None, 'dp', 'tensor')
- cross_out_grad: float32 [1024, 1024], P('dp', 'tensor')
- ffn_grad: float32 [2, 1024, 4096], P(None, 'dp', 'tensor')
- gains_grad: float32 [4, 1024], P(None, ('dp', 'tensor'))
- biases_grad: float32 [4, 1024], P(None, ('dp', 'tensor'))
The draws below stay inside these ranges and needn't reach their ends.
Inputs may be any that keep to these rules, and one draw needn't show every extreme that they name: `utt_lengths`: valid unit tokens of each utterance; at least one utterance fills all 512 slots. `enc_lengths`: valid encoder states of each utterance; at least one utterance fills all 256 slots.
All inputs are finite; a program needn't handle non-finite values.
Results may differ from the reference program's by a relative error of at most 0.035.
Values may be sent and summed in bfloat16 or wider, within the bound.
No kernel may reach another device: no remote copies, remote signals or barrier semaphores. Data moves between devices by JAX's collectives and lax.ppermute only.
A program may use at most 192 MiB of HBM per device.

```python
import jax
import jax.numpy as jnp
from jax import lax

D = 1024
HEADS = 16
HEAD_DIM = 64
FF = 4096
ROWS = 512
ENC = 256
TOKENS = 8192
ENC_TOKENS = 4096
N_DP = 16


def ragged_lengths(key, count, longest):
    picked = jax.random.randint(key, (), 0, count)
    drawn = jax.random.randint(jax.random.fold_in(key, 1), (count,), longest // 2, longest + 1)
    return jnp.where(jnp.arange(count) == picked, longest, drawn).astype(jnp.int32)


def draw_utt_lengths(key, part):
    key = jax.random.fold_in(key, 11)
    return ragged_lengths(key, N_DP, ROWS)


def draw_enc_lengths(key, part):
    key = jax.random.fold_in(key, 23)
    return ragged_lengths(key, N_DP, ENC)


def raised(values, stream_key, source, target, parts, factor):
    owner, partner = [(jnp.arange(values.shape[position]) // (values.shape[position] // parts)).reshape([-1 if axis == position else 1 for axis in range(values.ndim)]) for position in (source, target)]
    chosen = jax.random.permutation(stream_key, parts)[partner]
    strong = (owner == chosen) | (owner == (partner + parts // 2) % parts)
    return jnp.where(strong, factor * values, values)


def steps_of(key, dims, cuts, least, largest):
    factor_of, own = 1.0, jax.random.fold_in(key, 6)
    for dim, shards_of in cuts:
        draws = jnp.exp(jax.random.uniform(jax.random.fold_in(own, dim), (shards_of,), jnp.float32, least / len(cuts), largest / len(cuts)))
        factor_of = factor_of * jnp.repeat(draws, dims[dim] // shards_of).reshape([-1 if axis == dim else 1 for axis in range(len(dims))])
    return factor_of


def bell_draw(rng, dims, scale, most, shards=(), kind=jnp.bfloat16):
    level = steps_of(rng, dims, shards, -0.22, 0.18) if shards else 1.0
    values = jax.random.normal(rng, dims, jnp.float32) * scale * level
    return jnp.minimum(jnp.maximum(values, -most), most).astype(kind)


def gaussian_with(own_key, extent, deviation, limit, split, heavy, dtype=jnp.bfloat16):
    values = deviation * jax.random.normal(own_key, extent, jnp.float32)
    if split:
        values = values * steps_of(own_key, extent, split, -0.22, 0.18)
    return jnp.clip(raised(values, jax.random.fold_in(own_key, 3), *heavy), -limit, limit).astype(dtype)


def setup_inputs(seed: int = 0) -> dict:
    arg_keys = jax.random.split(jax.random.key(seed), 13)
    return {
        "tokens": gaussian_with(arg_keys[0], (TOKENS, D), 1.0, 12.0, ((0, 32),), (0, 1, 32, 2.75)),
        "enc_states": gaussian_with(arg_keys[1], (ENC_TOKENS, D), 1.0, 12.0, ((0, 32),), (0, 1, 32, 2.75)),
        "utt_lengths": draw_utt_lengths(jax.random.fold_in(arg_keys[12], 71), 0),
        "enc_lengths": draw_enc_lengths(jax.random.fold_in(arg_keys[12], 71), 0),
        "self_qkv": bell_draw(arg_keys[4], (3, D, D), D ** -0.5, 0.1875, ((1, 16), (2, 2))),
        "self_out": bell_draw(arg_keys[5], (D, D), (max(D * 4 // ROWS, 1)) ** -0.5, 2.0, ((0, 16), (1, 2))),
        "cross_qkv": bell_draw(arg_keys[6], (3, D, D), D ** -0.5, 0.1875, ((1, 16), (2, 2))),
        "cross_out": bell_draw(arg_keys[7], (D, D), (max(D * 4 // ENC, 1)) ** -0.5, 1.5, ((0, 16), (1, 2))),
        "ffn_proj": bell_draw(arg_keys[8], (2, D, FF), D ** -0.5, 0.1875, ((1, 16), (2, 2))),
        "norm_gains": jnp.clip(1.0 + 0.15 * jax.random.normal(arg_keys[9], (4, D), jnp.float32), 0.25, 1.75).astype(jnp.bfloat16),
        "norm_biases": bell_draw(arg_keys[10], (4, D), 0.2, 1.25, ((1, 16),)),
        "cotangent": gaussian_with(arg_keys[11], (TOKENS, D), 1.0, 12.0, ((0, 32),), (0, 1, 32, 2.75)),
    }


@jax.custom_vjp
def low(v):
    return lax.optimization_barrier(v.astype(jnp.bfloat16)).astype(jnp.float32)

@jax.custom_vjp
def low_back(v):
    return v

def low_keep(v):
    return (low(v), None)

def low_pass(kept, grad):
    return (grad,)

def back_keep(v):
    return (v, None)

def back_low(kept, grad):
    return (low(grad),)
low.defvjp(low_keep, low_pass)
low_back.defvjp(back_keep, back_low)
EPSILON = 1e-05
HIGH = lax.Precision.HIGHEST

def layer_norm(values, gain, shift):
    centre = lax.optimization_barrier(jnp.mean(values, axis=-1, keepdims=True))
    centred = values - centre
    spread = lax.optimization_barrier(jnp.mean(centred * centred, axis=-1, keepdims=True))
    return centred * lax.rsqrt(spread + EPSILON) * gain + shift

def attend(queries, keys, values, allowed):
    rows = queries.shape[0]
    count = keys.shape[0]
    query_heads = queries.reshape(rows, HEADS, HEAD_DIM)
    key_heads = keys.reshape(count, HEADS, HEAD_DIM)
    value_heads = values.reshape(count, HEADS, HEAD_DIM)
    scores = low_back(jnp.einsum('qhd,khd->hqk', query_heads, key_heads, precision=HIGH) * HEAD_DIM ** (-0.5))
    scores = jnp.where(allowed[None], scores, -1000000000.0)
    top = lax.optimization_barrier(jnp.max(scores, axis=-1, keepdims=True))
    exps = jnp.exp(scores - top)
    weights = low(exps / lax.optimization_barrier(jnp.sum(exps, axis=-1, keepdims=True)))
    mixed = jnp.einsum('hqk,khd->qhd', weights, value_heads, precision=HIGH)
    return low(low_back(mixed.reshape(rows, D)))

def project(values, weight):
    return low(low_back(jnp.dot(values, weight, precision=HIGH)))

def forward(token_block, encoded, self_qkv, self_out, cross_qkv, cross_out, ffn_proj, gains, shifts, length, enc_length):
    positions = jnp.arange(ROWS)
    causal = (positions[None, :] <= positions[:, None]) & (positions[None, :] < length)
    enc_positions = jnp.arange(ENC)
    reach = jnp.broadcast_to((enc_positions < enc_length)[None, :], (ROWS, ENC))
    normed = low(layer_norm(token_block, gains[0], shifts[0]))
    mixed = attend(project(normed, self_qkv[0]), project(normed, self_qkv[1]), project(normed, self_qkv[2]), causal)
    first = token_block + low_back(jnp.dot(mixed, self_out.T, precision=HIGH))
    normed = low(layer_norm(first, gains[1], shifts[1]))
    mixed = attend(project(normed, cross_qkv[0]), project(encoded, cross_qkv[1]), project(encoded, cross_qkv[2]), reach)
    second = first + low_back(jnp.dot(mixed, cross_out.T, precision=HIGH))
    normed = low(layer_norm(second, gains[2], shifts[2]))
    inner = low_back(jnp.dot(normed, ffn_proj[0], precision=HIGH))
    active = low(jax.nn.gelu(inner, approximate=True))
    third = second + low_back(jnp.dot(active, ffn_proj[1].T, precision=HIGH))
    return layer_norm(third, gains[3], shifts[3])

def reference(tokens, enc_states, utt_lengths, enc_lengths, self_qkv, self_out, cross_qkv, cross_out, ffn_proj, norm_gains, norm_biases, cotangent):
    params = (self_qkv, self_out, cross_qkv, cross_out, ffn_proj, norm_gains, norm_biases)
    params = tuple((item.astype(jnp.float32) for item in params))
    token_rows = tokens.astype(jnp.float32).reshape(N_DP, ROWS, D)
    enc_rows = enc_states.astype(jnp.float32).reshape(N_DP, ENC, D)
    cot_rows = cotangent.astype(jnp.float32).reshape(N_DP, ROWS, D)

    def one_utterance(totals, item):
        token_block, enc_block, cot_block, length, enc_length = item

        def apply(token_part, enc_part, *weights):
            return forward(token_part, enc_part, *weights, length, enc_length)
        result, pullback = jax.vjp(apply, token_block, enc_block, *params)
        valid = (jnp.arange(ROWS) < length)[:, None]
        grads = pullback(jnp.where(valid, cot_block, 0.0))
        totals = tuple((total + grad for total, grad in zip(totals, grads[2:])))
        return (totals, (result.astype(jnp.bfloat16), grads[0], grads[1]))
    start = tuple((jnp.zeros_like(item) for item in params))
    totals, (outputs, token_grads, enc_grads) = lax.scan(one_utterance, start, (token_rows, enc_rows, cot_rows, utt_lengths, enc_lengths))
    return (outputs.reshape(TOKENS, D), token_grads.reshape(TOKENS, D), enc_grads.reshape(ENC_TOKENS, D), totals[0], totals[1], totals[2], totals[3], totals[4], totals[5], totals[6])
```

```python
import jax
import jax.numpy as jnp
from jax import lax
from jax.sharding import PartitionSpec as P

HEAD_DIM = 64
EPSILON = 1e-05
NEG_FILL = -1000000000.0
BF = jnp.bfloat16
F32 = jnp.float32


def dot(a, b, dims):
    return lax.dot_general(a, b, (dims, ((), ())), preferred_element_type=F32)


def mm(a, b):
    return dot(a, b, ((1,), (0,)))


def mm_t(a, b):
    return dot(a, b, ((1,), (1,)))


def t_mm(a, b):
    return dot(a, b, ((0,), (0,)))


def swap(values):
    return lax.ppermute(values, "tensor", [(0, 1), (1, 0)])


def normalize(values):
    centre = jnp.mean(values, axis=-1, keepdims=True)
    centred = values - centre
    spread = jnp.mean(centred * centred, axis=-1, keepdims=True)
    rstd = lax.rsqrt(spread + EPSILON)
    return centred * rstd, rstd


def norm_back(hat, rstd, gain, grad):
    scaled = grad * gain
    first = jnp.mean(scaled, axis=-1, keepdims=True)
    second = jnp.mean(scaled * hat, axis=-1, keepdims=True)
    return (
        rstd * (scaled - first - hat * second),
        jnp.sum(grad * hat, axis=0),
        jnp.sum(grad, axis=0),
    )


def gelu_both(z):
    c = 0.7978845608028654
    t = jnp.tanh(c * (z + 0.044715 * z * z * z))
    value = 0.5 * z * (1.0 + t)
    slope = 0.5 * (1.0 + t) + 0.5 * z * (1.0 - t * t) * c * (1.0 + 3.0 * 0.044715 * z * z)
    return value, slope


def heads_of(values):
    rows, cols = values.shape
    return values.reshape(rows, cols // HEAD_DIM, HEAD_DIM)


def attend(q, k, v, allowed):
    scale = HEAD_DIM ** (-0.5)
    scores = (
        jnp.einsum("qhd,khd->hqk", heads_of(q), heads_of(k), preferred_element_type=F32) * scale
    )
    scores = jnp.where(allowed[None], scores, NEG_FILL)
    top = jnp.max(scores, axis=-1, keepdims=True)
    exps = jnp.exp(scores - top)
    total = jnp.sum(exps, axis=-1, keepdims=True)
    weights = (exps / total).astype(BF)
    mixed = jnp.einsum("hqk,khd->qhd", weights, heads_of(v), preferred_element_type=F32)
    return mixed.astype(BF).reshape(q.shape), top + jnp.log(total)


def attend_back(q, k, v, grad, logs, allowed):
    scale = HEAD_DIM ** (-0.5)
    qh, kh, vh, gh = heads_of(q), heads_of(k), heads_of(v), heads_of(grad)
    scores = jnp.einsum("qhd,khd->hqk", qh, kh, preferred_element_type=F32) * scale
    scores = jnp.where(allowed[None], scores, NEG_FILL)
    probs = jnp.exp(scores - logs)
    dv = jnp.einsum("hqk,qhd->khd", probs.astype(BF), gh, preferred_element_type=F32)
    dprobs = jnp.einsum("qhd,khd->hqk", gh, vh, preferred_element_type=F32)
    inner = jnp.sum(dprobs * probs, axis=-1, keepdims=True)
    ds = (probs * (dprobs - inner)).astype(BF)
    dq = jnp.einsum("hqk,khd->qhd", ds, kh, preferred_element_type=F32) * scale
    dk = jnp.einsum("hqk,qhd->khd", ds, qh, preferred_element_type=F32) * scale
    return (
        dq.astype(BF).reshape(q.shape),
        dk.astype(BF).reshape(k.shape),
        dv.astype(BF).reshape(v.shape),
    )


def make_body(n_dp):
    bits = n_dp.bit_length() - 1
    assert n_dp == 1 << bits

    def hop(values, bit):
        return lax.ppermute(values, "dp", [(i, i ^ (1 << bit)) for i in range(n_dp)])

    far = tuple(range(bits - 1, 1, -1))
    gather_a = far + (1, 0)
    gather_b = far + (0, 1)
    gather_c = (0, 1) + far
    gather_d = (1, 0) + far
    scatter_a, scatter_b, scatter_c, scatter_d = (
        order[::-1] for order in (gather_a, gather_b, gather_c, gather_d)
    )

    def gather(shard, order):
        lead, feats, *rest = shard.shape
        held = shard.reshape((lead,) + (1,) * bits + (feats, *rest))
        for bit in order:
            held = jnp.concatenate([held, hop(held, bit)], axis=1 + bit)
        return held.reshape(lead, n_dp * feats, *rest)

    def scatter(full, order, kind):
        lead, feats, *rest = full.shape
        held = full.reshape((lead,) + (2,) * bits + (feats // n_dp, *rest))
        for count, bit in enumerate(order):
            keep = lax.slice_in_dim(held, 0, 1, axis=1 + bit)
            send = lax.slice_in_dim(held, 1, 2, axis=1 + bit)
            total = keep.astype(F32) + hop(send, bit).astype(F32)
            held = total.astype(F32 if count == bits - 1 else kind)
        return held.reshape(lead, feats // n_dp, *rest)

    def body(
        tokens,
        enc_states,
        utt_lengths,
        enc_lengths,
        self_qkv,
        self_out,
        cross_qkv,
        cross_out,
        ffn_proj,
        norm_gains,
        norm_biases,
        cotangent,
    ):
        local, width = tokens.shape
        enc_local = enc_states.shape[0]
        rows = 2 * local
        count = 2 * enc_local
        units = ffn_proj.shape[2]
        half = units // 2
        length = utt_lengths[0]
        enc_length = enc_lengths[0]
        core = lax.axis_index("tensor")
        me = lax.axis_index("dp")

        block = width // n_dp
        cols = jnp.arange(width, dtype=jnp.int32)
        labels = cols // block
        reverse = jnp.zeros_like(labels)
        for bit in range(bits):
            reverse = reverse | (((labels >> (bits - 1 - bit)) & 1) << bit)
        source = (me ^ reverse) * block + cols % block
        relabel = (cols[:, None] == source[None, :]).astype(BF)

        params = jnp.concatenate([norm_gains, norm_biases])
        params = gather(params.astype(BF), gather_a).astype(F32)
        gains, shifts = params[:4], params[4:]

        w_qk = gather(self_qkv[:2], gather_a)
        w_vo = gather(jnp.stack([self_qkv[2], self_out]), gather_b)
        c_kv = gather(cross_qkv[1:], gather_a)
        c_qo = gather(jnp.stack([cross_qkv[0], cross_out]), gather_b)
        up = [
            gather(ffn_proj[:1, :, :half], gather_a)[0],
            gather(ffn_proj[:1, :, half:], gather_b)[0],
        ]
        down = [
            gather(ffn_proj[1:, :, :half], gather_c)[0],
            gather(ffn_proj[1:, :, half:], gather_d)[0],
        ]

        def whole(mine):
            other = swap(mine)
            return jnp.where(
                core == 0,
                jnp.concatenate([mine, other]),
                jnp.concatenate([other, mine]),
            )

        def relabeled(values):
            return mm(values, relabel).astype(BF)

        def own(values):
            size = values.shape[0] // 2
            return lax.dynamic_slice_in_dim(values, core * size, size)

        def other(values):
            size = values.shape[0] // 2
            return lax.dynamic_slice_in_dim(values, (1 - core) * size, size)

        def restored(values):
            return lax.dot_general(
                values,
                relabel.astype(F32),
                (((1,), (1,)), ((), ())),
                precision=lax.Precision.HIGHEST,
                preferred_element_type=F32,
            )

        def both(part):
            mine = part.astype(BF)
            return mine.astype(F32) + swap(mine).astype(F32)

        x0 = whole(relabeled(tokens)).astype(F32)
        enc = whole(relabeled(enc_states))
        cot = whole(relabeled(cotangent)).astype(F32)

        position = jnp.arange(rows, dtype=jnp.int32)
        enc_position = jnp.arange(count, dtype=jnp.int32)
        causal = (position[None, :] <= position[:, None]) & (position[None, :] < length)
        reach = jnp.broadcast_to((enc_position < enc_length)[None, :], (rows, count))

        hat0, rstd0 = normalize(x0)
        normed1 = (hat0 * gains[0] + shifts[0]).astype(BF)
        q1 = mm(normed1, w_qk[0]).astype(BF)
        k1 = mm(normed1, w_qk[1]).astype(BF)
        v1 = mm(normed1, w_vo[0]).astype(BF)
        o1, logs1 = attend(q1, k1, v1, causal)
        x1 = x0 + both(mm_t(o1, w_vo[1]))
        hat1, rstd1 = normalize(x1)
        normed2 = (hat1 * gains[1] + shifts[1]).astype(BF)
        k2 = mm(enc, c_kv[0]).astype(BF)
        v2 = mm(enc, c_kv[1]).astype(BF)
        q2 = mm(normed2, c_qo[0]).astype(BF)
        o2, logs2 = attend(q2, k2, v2, reach)
        x2 = x1 + both(mm_t(o2, c_qo[1]))
        hat2, rstd2 = normalize(x2)
        normed3 = (hat2 * gains[2] + shifts[2]).astype(BF)
        acts, slopes = [], []
        for w in up:
            value, slope = gelu_both(mm(normed3, w))
            acts.append(value.astype(BF))
            slopes.append(slope)
        x3 = x2 + both(mm_t(acts[0], down[0]) + mm_t(acts[1], down[1]))
        hat3, rstd3 = normalize(x3)
        output = restored(own(hat3 * gains[3] + shifts[3]).astype(BF).astype(F32)).astype(BF)
        gout = cot * (position < length)[:, None]
        dx3, dgain3, dshift3 = norm_back(hat3, rstd3, gains[3], gout)
        dy3 = dx3.astype(BF)
        d_down = [t_mm(dy3, a).astype(BF)[None] for a in acts]
        s_down = [scatter(d_down[0], scatter_c, BF), scatter(d_down[1], scatter_d, BF)]
        dus = [(mm(dy3, w) * s).astype(BF) for w, s in zip(down, slopes)]
        d_up = [t_mm(normed3, du).astype(BF)[None] for du in dus]
        s_up = [scatter(d_up[0], scatter_a, BF), scatter(d_up[1], scatter_b, BF)]
        dn3 = both(mm_t(dus[0], up[0]) + mm_t(dus[1], up[1]))
        back, dgain2, dshift2 = norm_back(hat2, rstd2, gains[2], dn3)
        dx2 = dx3 + back
        dy2 = dx2.astype(BF)
        d_cross_out = t_mm(dy2, o2).astype(BF)
        do2 = mm(dy2, c_qo[1]).astype(BF)
        dq2, dk2, dv2 = attend_back(q2, k2, v2, do2, logs2, reach)
        s_qo = scatter(jnp.stack([t_mm(normed2, dq2).astype(BF), d_cross_out]), scatter_a, BF)
        s_kv = scatter(
            jnp.stack([t_mm(enc, dk2).astype(BF), t_mm(enc, dv2).astype(BF)]), scatter_b, BF
        )
        enc_part = mm_t(dk2, c_kv[0]) + mm_t(dv2, c_kv[1])
        enc_grad = restored(own(enc_part) + swap(other(enc_part).astype(BF)).astype(F32))
        dn2 = both(mm_t(dq2, c_qo[0]))
        back, dgain1, dshift1 = norm_back(hat1, rstd1, gains[1], dn2)
        dx1 = dx2 + back
        dy1 = dx1.astype(BF)
        d_self_out = t_mm(dy1, o1).astype(BF)
        do1 = mm(dy1, w_vo[1]).astype(BF)
        dq1, dk1, dv1 = attend_back(q1, k1, v1, do1, logs1, causal)
        t_vo = scatter(jnp.stack([t_mm(normed1, dv1).astype(BF), d_self_out]), scatter_a, BF)
        t_qk = scatter(
            jnp.stack([t_mm(normed1, dq1).astype(BF), t_mm(normed1, dk1).astype(BF)]),
            scatter_b,
            BF,
        )
        dn1 = both(mm_t(dq1, w_qk[0]) + mm_t(dk1, w_qk[1]) + mm_t(dv1, w_vo[0]))
        back, dgain0, dshift0 = norm_back(hat0, rstd0, gains[0], dn1)
        token_grad = restored(own(dx1 + back))

        terms = jnp.stack(
            [dgain0, dgain1, dgain2, dgain3, dshift0, dshift1, dshift2, dshift3]
        )
        terms = scatter(terms, scatter_a, F32)
        part = terms.shape[1] // 2
        terms = lax.dynamic_slice_in_dim(terms, core * part, part, axis=1)
        return (
            output,
            token_grad,
            enc_grad,
            jnp.concatenate([t_qk, t_vo[:1]]),
            t_vo[1],
            jnp.concatenate([s_qo[:1], s_kv]),
            s_qo[1],
            jnp.concatenate(
                [jnp.concatenate(s_up, axis=2), jnp.concatenate(s_down, axis=2)]
            ),
            terms[:4],
            terms[4:],
        )

    return body


def solution(mesh):
    return jax.shard_map(
        make_body(mesh.shape["dp"]),
        mesh=mesh,
        in_specs=(
            P(("dp", "tensor"), None),
            P(("dp", "tensor"), None),
            P("dp"),
            P("dp"),
            P(None, "dp", "tensor"),
            P("dp", "tensor"),
            P(None, "dp", "tensor"),
            P("dp", "tensor"),
            P(None, "dp", "tensor"),
            P(None, "dp"),
            P(None, "dp"),
            P(("dp", "tensor"), None),
        ),
        out_specs=(
            P(("dp", "tensor"), None),
            P(("dp", "tensor"), None),
            P(("dp", "tensor"), None),
            P(None, "dp", "tensor"),
            P("dp", "tensor"),
            P(None, "dp", "tensor"),
            P("dp", "tensor"),
            P(None, "dp", "tensor"),
            P(None, ("dp", "tensor")),
            P(None, ("dp", "tensor")),
        ),
        check_vma=False,
    )
```

```python
import jax
import jax.numpy as jnp
from jax import lax
from jax.sharding import PartitionSpec as P

HEAD_DIM = 64
EPSILON = 1e-05
NEG_FILL = -1000000000.0
BF = jnp.bfloat16
F32 = jnp.float32


def dot(a, b, dims):
    return lax.dot_general(a, b, (dims, ((), ())), preferred_element_type=F32)


def mm(a, b):
    return dot(a, b, ((1,), (0,)))


def mm_t(a, b):
    return dot(a, b, ((1,), (1,)))


def t_mm(a, b):
    return dot(a, b, ((0,), (0,)))


def swap(values):
    return lax.ppermute(values, "tensor", [(0, 1), (1, 0)])


def normalize(values):
    centre = jnp.mean(values, axis=-1, keepdims=True)
    centred = values - centre
    spread = jnp.mean(centred * centred, axis=-1, keepdims=True)
    rstd = lax.rsqrt(spread + EPSILON)
    return centred * rstd, rstd


def norm_back(hat, rstd, gain, grad):
    scaled = grad * gain
    first = jnp.mean(scaled, axis=-1, keepdims=True)
    second = jnp.mean(scaled * hat, axis=-1, keepdims=True)
    return (
        rstd * (scaled - first - hat * second),
        jnp.sum(grad * hat, axis=0),
        jnp.sum(grad, axis=0),
    )


def gelu_both(z):
    c = 0.7978845608028654
    t = jnp.tanh(c * (z + 0.044715 * z * z * z))
    value = 0.5 * z * (1.0 + t)
    slope = 0.5 * (1.0 + t) + 0.5 * z * (1.0 - t * t) * c * (1.0 + 3.0 * 0.044715 * z * z)
    return value, slope


def heads_of(values):
    rows, cols = values.shape
    return values.reshape(rows, cols // HEAD_DIM, HEAD_DIM)


def attend(q, k, v, allowed):
    scale = HEAD_DIM ** (-0.5)
    scores = (
        jnp.einsum("qhd,khd->hqk", heads_of(q), heads_of(k), preferred_element_type=F32) * scale
    )
    scores = jnp.where(allowed[None], scores, NEG_FILL)
    top = jnp.max(scores, axis=-1, keepdims=True)
    exps = jnp.exp(scores - top)
    total = jnp.sum(exps, axis=-1, keepdims=True)
    weights = (exps / total).astype(BF)
    mixed = jnp.einsum("hqk,khd->qhd", weights, heads_of(v), preferred_element_type=F32)
    return mixed.astype(BF).reshape(q.shape), top + jnp.log(total)


def attend_back(q, k, v, grad, logs, allowed):
    scale = HEAD_DIM ** (-0.5)
    qh, kh, vh, gh = heads_of(q), heads_of(k), heads_of(v), heads_of(grad)
    scores = jnp.einsum("qhd,khd->hqk", qh, kh, preferred_element_type=F32) * scale
    scores = jnp.where(allowed[None], scores, NEG_FILL)
    probs = jnp.exp(scores - logs)
    dv = jnp.einsum("hqk,qhd->khd", probs.astype(BF), gh, preferred_element_type=F32)
    dprobs = jnp.einsum("qhd,khd->hqk", gh, vh, preferred_element_type=F32)
    inner = jnp.sum(dprobs * probs, axis=-1, keepdims=True)
    ds = (probs * (dprobs - inner)).astype(BF)
    dq = jnp.einsum("hqk,khd->qhd", ds, kh, preferred_element_type=F32) * scale
    dk = jnp.einsum("hqk,qhd->khd", ds, qh, preferred_element_type=F32) * scale
    return (
        dq.astype(BF).reshape(q.shape),
        dk.astype(BF).reshape(k.shape),
        dv.astype(BF).reshape(v.shape),
    )


def behind(values, earlier):
    return lax.optimization_barrier((values, earlier))[0]


def make_body(n_dp):
    bits = n_dp.bit_length() - 1
    assert n_dp == 1 << bits

    def hop(values, bit):
        return lax.ppermute(values, "dp", [(i, i ^ (1 << bit)) for i in range(n_dp)])

    far = range(bits - 1, 1, -1)

    def gather_far(held, bits_now, after):
        for bit in bits_now:
            after = hop(behind(held, after), bit)
            held = jnp.stack([held, after])
        return held, after

    def inner_rows(v, start, stop):
        return lax.slice_in_dim(v, start, stop, axis=v.ndim - 2)

    def gather_sides(held, after):
        held = behind(held, after)
        return hop(held, 0), hop(held, 1)

    def gather_corner(by_x, by_y, cut, after):
        first = behind(inner_rows(by_y, 0, cut), after)
        second = behind(inner_rows(by_x, cut, by_x.shape[-2]), after)
        return hop(first, 0), hop(second, 1)

    def gathered(held, sides, corner, cut):
        (by_x, by_y), (first, second) = sides, corner

        def rows(start, stop):
            last, offset = (first, 0) if stop <= cut else (second, cut)
            parts = [inner_rows(v, start, stop) for v in (held, by_y, by_x)]
            parts.append(inner_rows(last, start - offset, stop - offset))
            return jnp.concatenate(
                [v.reshape(-1, stop - start, v.shape[-1]) for v in parts]
            )

        return rows

    def full_weight(rows, start, stop):
        return rows(start, stop).reshape(-1, rows(start, stop).shape[-1])

    def scatter_near(one, two, after):
        quarter = one.shape[0] // 4
        part = lambda v, label: lax.slice_in_dim(v, label * quarter, (label + 1) * quarter)
        plus = lambda v, w: (v.astype(F32) + w.astype(F32)).astype(BF)
        corner_one, corner_two = behind((part(one, 3), part(two, 3)), after)
        got_one, got_two = hop(corner_one, 0), hop(corner_two, 1)
        for_y = jnp.stack([plus(part(one, 1), got_one), part(two, 1)])
        for_x = jnp.stack([part(one, 2), plus(part(two, 2), got_two)])
        got_x, got_y = hop(for_x, 0), hop(for_y, 1)
        own = jnp.stack([part(one, 0), part(two, 0)])
        total = (own.astype(F32) + got_x.astype(F32) + got_y.astype(F32)).astype(BF)
        return total, (got_x, got_y)

    def scatter_far(held, after):
        parts, feats, cols = held.shape
        held = held.reshape(parts, -1, feats * 4 // n_dp, cols)
        for count, bit in enumerate(reversed(far)):
            middle = held.shape[1] // 2
            send = behind(held[:, middle:], after)
            after = hop(send, bit)
            held = held[:, :middle].astype(F32) + after.astype(F32)
            if count < len(far) - 1:
                held = held.astype(BF)
        return held[:, 0], after

    planes = [[4 * z + p for p in range(4)] for z in range(n_dp // 4)]
    lines = [[4 * z + p for z in range(n_dp // 4)] for p in range(4)]
    plane_first = [chip for line in lines for chip in line]

    def sum_plane(full):
        return lax.psum_scatter(
            full, "dp", scatter_dimension=0, tiled=True, axis_index_groups=planes
        )

    def sum_lines(full):
        return lax.psum_scatter(
            full, "dp", scatter_dimension=0, tiled=True, axis_index_groups=lines
        )

    def scatter_small(full):
        lead, feats = full.shape
        held = full.reshape((lead,) + (2,) * bits + (feats // n_dp,))
        for bit in range(bits):
            keep = lax.index_in_dim(held, 0, 1, keepdims=False)
            held = keep + hop(lax.index_in_dim(held, 1, 1, keepdims=False), bit)
        return held

    def body(
        tokens,
        enc_states,
        utt_lengths,
        enc_lengths,
        self_qkv,
        self_out,
        cross_qkv,
        cross_out,
        ffn_proj,
        norm_gains,
        norm_biases,
        cotangent,
    ):
        local, width = tokens.shape
        enc_local = enc_states.shape[0]
        rows = 2 * local
        count = 2 * enc_local
        units = ffn_proj.shape[2]
        length = utt_lengths[0]
        enc_length = enc_lengths[0]
        core = lax.axis_index("tensor")
        me = lax.axis_index("dp")

        block = width // n_dp
        cols = jnp.arange(width, dtype=jnp.int32)
        labels = cols // block
        reverse = jnp.zeros_like(labels)
        for bit in range(bits):
            reverse = reverse | (((labels >> (bits - 1 - bit)) & 1) << bit)
        source = (me ^ reverse) * block + cols % block
        relabel = (cols[:, None] == source[None, :]).astype(BF)
        chip = source // block
        placed = ((chip & 3) * (n_dp // 4) + (chip >> 2)) * block + cols % block
        replace = (placed[:, None] == cols[None, :]).astype(BF)

        feats = norm_gains.shape[1]
        beside = lambda *v: jnp.concatenate(v, axis=-1)
        above = lambda *v: jnp.concatenate(v)
        params = jnp.concatenate([norm_gains, norm_biases]).reshape(1, 8 * feats)
        params = jnp.pad(params, ((0, 7), (0, 2 * self_out.shape[1] - 8 * feats)))
        ffn = lax.all_gather(
            ffn_proj, "dp", axis=1, tiled=True, axis_index_groups=[plane_first]
        )
        up, down = ffn[0], ffn[1]
        s_a = above(beside(self_qkv[0], self_qkv[1]), beside(self_qkv[2], self_out), params)
        s_c = above(beside(cross_qkv[1], cross_qkv[2]), beside(cross_qkv[0], cross_out))
        held_a, token = gather_far(s_a, far, norm_gains)
        sides_a = gather_sides(held_a, token)
        held_c, token = gather_far(s_c, far[:-1], token)
        token = (token, sides_a)
        corner_a = gather_corner(*sides_a, feats, token)
        held_c, token = gather_far(held_c, far[-1:], token)
        token = (token, corner_a)
        sides_c = gather_sides(held_c, token)
        corner_c = gather_corner(*sides_c, feats, sides_c)
        weights = [
            gathered(held_a, sides_a, corner_a, feats),
            gathered(held_c, sides_c, corner_c, feats),
        ]
        w_qk, w_vo = full_weight(weights[0], 0, feats), full_weight(weights[0], feats, 2 * feats)
        params = weights[0](2 * feats, 2 * feats + 8)[:, 0, : 8 * feats]
        params = params.reshape(n_dp, 8, feats).transpose(1, 0, 2).reshape(8, width).astype(F32)
        gains, shifts = params[:4], params[4:]
        c_kv, c_qo = [full_weight(weights[1], i * feats, (i + 1) * feats) for i in (0, 1)]
        inner_cols = self_out.shape[1]
        w_v, w_o = w_vo[:, :inner_cols], w_vo[:, inner_cols:]
        c_q, c_o = c_qo[:, :inner_cols], c_qo[:, inner_cols:]

        def whole(mine):
            other = swap(mine)
            return jnp.where(
                core == 0,
                jnp.concatenate([mine, other]),
                jnp.concatenate([other, mine]),
            )

        def relabeled(values):
            return mm(values, relabel).astype(BF)

        def own(values):
            size = values.shape[0] // 2
            return lax.dynamic_slice_in_dim(values, core * size, size)

        def other(values):
            size = values.shape[0] // 2
            return lax.dynamic_slice_in_dim(values, (1 - core) * size, size)

        def restored(values):
            return lax.dot_general(
                values,
                relabel.astype(F32),
                (((1,), (1,)), ((), ())),
                precision=lax.Precision.HIGHEST,
                preferred_element_type=F32,
            )

        def both(part):
            mine = part.astype(BF)
            return mine.astype(F32) + swap(mine).astype(F32)

        x0 = whole(relabeled(tokens)).astype(F32)
        enc = whole(relabeled(enc_states))
        cot = whole(relabeled(cotangent)).astype(F32)

        position = jnp.arange(rows, dtype=jnp.int32)
        enc_position = jnp.arange(count, dtype=jnp.int32)
        causal = (position[None, :] <= position[:, None]) & (position[None, :] < length)
        reach = jnp.broadcast_to((enc_position < enc_length)[None, :], (rows, count))

        hat0, rstd0 = normalize(x0)
        normed1 = (hat0 * gains[0] + shifts[0]).astype(BF)
        qk1 = mm(normed1, w_qk).astype(BF)
        q1, k1 = qk1[:, :inner_cols], qk1[:, inner_cols:]
        v1 = mm(normed1, w_v).astype(BF)
        o1, logs1 = attend(q1, k1, v1, causal)
        x1 = x0 + both(mm_t(o1, w_o))
        hat1, rstd1 = normalize(x1)
        normed2 = (hat1 * gains[1] + shifts[1]).astype(BF)
        kv2 = mm(enc, c_kv).astype(BF)
        k2, v2 = kv2[:, :inner_cols], kv2[:, inner_cols:]
        q2 = mm(normed2, c_q).astype(BF)
        o2, logs2 = attend(q2, k2, v2, reach)
        x2 = x1 + both(mm_t(o2, c_o))
        hat2, rstd2 = normalize(x2)
        normed3 = (hat2 * gains[2] + shifts[2]).astype(BF)
        normed3 = mm(normed3, replace).astype(BF)
        act, slope = gelu_both(mm(normed3, up))
        act = act.astype(BF)
        x3 = x2 + both(mm_t(mm_t(act, down).astype(BF), replace))
        hat3, rstd3 = normalize(x3)
        output = restored(own(hat3 * gains[3] + shifts[3]).astype(BF).astype(F32)).astype(BF)
        gout = cot * (position < length)[:, None]
        dx3, dgain3, dshift3 = norm_back(hat3, rstd3, gains[3], gout)
        dy3 = dx3.astype(BF)
        dy3_there = mm(dy3, replace).astype(BF)
        s_down = sum_plane(t_mm(dy3_there, act).astype(BF))
        du = (mm(dy3_there, down) * slope).astype(BF)
        s_up = sum_plane(t_mm(normed3, du).astype(BF))
        s_ffn = sum_lines(jnp.concatenate([s_up, s_down], axis=1))
        dn3 = both(mm_t(mm_t(du, up).astype(BF), replace))
        back, dgain2, dshift2 = norm_back(hat2, rstd2, gains[2], dn3)
        dx2 = dx3 + back
        dy2 = dx2.astype(BF)
        do2 = mm(dy2, c_o).astype(BF)
        dq2, dk2, dv2 = attend_back(q2, k2, v2, do2, logs2, reach)
        dkv2 = beside(dk2, dv2)
        s_cross, near = scatter_near(
            t_mm(enc, dkv2).astype(BF),
            beside(t_mm(normed2, dq2).astype(BF), t_mm(dy2, o2).astype(BF)),
            dy3,
        )
        enc_part = mm_t(dkv2, c_kv)
        enc_grad = restored(own(enc_part) + swap(other(enc_part).astype(BF)).astype(F32))
        dn2 = both(mm_t(dq2, c_q))
        back, dgain1, dshift1 = norm_back(hat1, rstd1, gains[1], dn2)
        dx1 = dx2 + back
        dy1 = dx1.astype(BF)
        do1 = mm(dy1, w_o).astype(BF)
        dq1, dk1, dv1 = attend_back(q1, k1, v1, do1, logs1, causal)
        dqk1 = beside(dq1, dk1)
        s_self, near = scatter_near(
            t_mm(normed1, dqk1).astype(BF),
            beside(t_mm(normed1, dv1).astype(BF), t_mm(dy1, o1).astype(BF)),
            near,
        )
        dn1 = both(mm_t(dqk1, w_qk) + mm_t(dv1, w_v))
        back, dgain0, dshift0 = norm_back(hat0, rstd0, gains[0], dn1)
        token_grad = restored(own(dx1 + back))

        s_cross, last = scatter_far(s_cross, dy3)
        s_self, last = scatter_far(s_self, last)
        terms = jnp.stack(
            [dgain0, dgain1, dgain2, dgain3, dshift0, dshift1, dshift2, dshift3]
        )
        terms = scatter_small(terms)
        part = terms.shape[1] // 2
        terms = lax.dynamic_slice_in_dim(terms, core * part, part, axis=1)
        left = lambda v: v[:, :inner_cols]
        right = lambda v: v[:, inner_cols:]
        return (
            output,
            token_grad,
            enc_grad,
            jnp.stack([left(s_self[0]), right(s_self[0]), left(s_self[1])]),
            right(s_self[1]),
            jnp.stack([left(s_cross[1]), left(s_cross[0]), right(s_cross[0])]),
            right(s_cross[1]),
            jnp.stack([s_ffn[:, :units], s_ffn[:, units:]]).astype(F32),
            terms[:4],
            terms[4:],
        )

    return body


def solution(mesh):
    return jax.shard_map(
        make_body(mesh.shape["dp"]),
        mesh=mesh,
        in_specs=(
            P(("dp", "tensor"), None),
            P(("dp", "tensor"), None),
            P("dp"),
            P("dp"),
            P(None, "dp", "tensor"),
            P("dp", "tensor"),
            P(None, "dp", "tensor"),
            P("dp", "tensor"),
            P(None, "dp", "tensor"),
            P(None, "dp"),
            P(None, "dp"),
            P(("dp", "tensor"), None),
        ),
        out_specs=(
            P(("dp", "tensor"), None),
            P(("dp", "tensor"), None),
            P(("dp", "tensor"), None),
            P(None, "dp", "tensor"),
            P("dp", "tensor"),
            P(None, "dp", "tensor"),
            P("dp", "tensor"),
            P(None, "dp", "tensor"),
            P(None, ("dp", "tensor")),
            P(None, ("dp", "tensor")),
        ),
        check_vma=False,
    )
```

```python
import functools

import jax
import jax.numpy as jnp
from jax import lax
from jax.experimental import pallas as pl
from jax.experimental.pallas import tpu as pltpu
from jax.sharding import PartitionSpec as P

HEAD_DIM = 64
EPSILON = 1e-05
NEG_FILL = -1000000000.0
BF = jnp.bfloat16
F32 = jnp.float32


def dot(a, b, dims):
    return lax.dot_general(a, b, (dims, ((), ())), preferred_element_type=F32)


def mm(a, b):
    return dot(a, b, ((1,), (0,)))


def mm_t(a, b):
    return dot(a, b, ((1,), (1,)))


def t_mm(a, b):
    return dot(a, b, ((0,), (0,)))


def swap(values):
    return lax.ppermute(values, "tensor", [(0, 1), (1, 0)])


def normalize(values):
    centre = jnp.mean(values, axis=-1, keepdims=True)
    centred = values - centre
    spread = jnp.mean(centred * centred, axis=-1, keepdims=True)
    rstd = lax.rsqrt(spread + EPSILON)
    return centred * rstd, rstd


def gelu_both(z):
    c = 0.7978845608028654
    t = jnp.tanh(c * (z + 0.044715 * z * z * z))
    value = 0.5 * z * (1.0 + t)
    slope = 0.5 * (1.0 + t) + 0.5 * z * (1.0 - t * t) * c * (1.0 + 3.0 * 0.044715 * z * z)
    return value, slope


def masked(values, head):
    lane = lax.broadcasted_iota(jnp.int32, values.shape, 1)
    return jnp.where((lane < HEAD_DIM) == (head == 0), values, jnp.zeros_like(values))


def scores_of(keys, queries, start, limit, causal):
    raw = mm_t(keys, queries)
    key = lax.broadcasted_iota(jnp.int32, raw.shape, 0)
    allowed = key < limit
    if causal:
        query = start + lax.broadcasted_iota(jnp.int32, raw.shape, 1)
        allowed = allowed & (key <= query)
    return jnp.where(allowed, raw, NEG_FILL)


def blocks_of(rows, count, causal):
    if causal:
        half = rows // 2
        return [(0, half, half), (half, half, count)]
    return [(0, rows, count)]


def forward_kernel(causal, limit_ref, q_ref, k_ref, v_ref, out_ref, log_ref):
    limit = limit_ref[0]
    scale = HEAD_DIM ** (-0.5)
    for start, size, reach in blocks_of(q_ref.shape[0], k_ref.shape[0], causal):
        queries = (q_ref[start : start + size, :].astype(F32) * scale).astype(BF)
        mixed = None
        for head in range(2):
            keys = masked(k_ref[:reach, :], head)
            values = masked(v_ref[:reach, :], head)
            scores = scores_of(keys, queries, start, limit, causal)
            top = jnp.max(scores, axis=0, keepdims=True)
            exps = jnp.exp(scores - top)
            total = jnp.sum(exps, axis=0, keepdims=True)
            probs = (exps * (1.0 / total)).astype(BF)
            part = t_mm(probs, values)
            mixed = part if mixed is None else mixed + part
            log_ref[0, head : head + 1, start : start + size] = top + jnp.log(total)
        out_ref[start : start + size, :] = mixed.astype(BF)


def backward_kernel(
    causal, limit_ref, q_ref, k_ref, v_ref, do_ref, log_ref, dq_ref, dk_ref, dv_ref, sk, sv
):
    limit = limit_ref[0]
    scale = HEAD_DIM ** (-0.5)
    sk[...] = jnp.zeros_like(sk)
    sv[...] = jnp.zeros_like(sv)
    for start, size, reach in blocks_of(q_ref.shape[0], k_ref.shape[0], causal):
        queries = (q_ref[start : start + size, :].astype(F32) * scale).astype(BF)
        grad = do_ref[start : start + size, :]
        total = None
        for head in range(2):
            keys = masked(k_ref[:reach, :], head)
            values = masked(v_ref[:reach, :], head)
            scores = scores_of(keys, queries, start, limit, causal)
            probs = jnp.exp(scores - log_ref[0, head : head + 1, start : start + size])
            sv[:reach, :] += mm(probs.astype(BF), masked(grad, head))
            dprobs = mm_t(values, grad)
            inner = jnp.sum(dprobs * probs, axis=0, keepdims=True)
            ds = (probs * (dprobs - inner)).astype(BF)
            sk[:reach, :] += mm(ds, masked(queries, head))
            part = t_mm(ds, keys)
            total = part if total is None else total + part
        dq_ref[start : start + size, :] = (total * scale).astype(BF)
    dk_ref[...] = sk[...].astype(BF)
    dv_ref[...] = sv[...].astype(BF)


VMEM_LIMIT = 16 * 1024 * 1024


def params_of():
    return pltpu.CompilerParams(
        dimension_semantics=("arbitrary",), vmem_limit_bytes=VMEM_LIMIT
    )


def column_spec(rows, offset):
    return pl.BlockSpec((rows, 2 * HEAD_DIM), lambda i: (0, i + offset))


def log_spec(rows):
    return pl.BlockSpec((1, 2, rows), lambda i: (i, 0, 0))


SCALAR = pl.BlockSpec(memory_space=pltpu.SMEM)


def attend(limit, q, k, v, cols, causal):
    pairs = cols // (2 * HEAD_DIM)
    rows, count = q[0].shape[0], k[0].shape[0]
    work = rows * count * cols
    return pl.pallas_call(
        functools.partial(forward_kernel, causal),
        grid=(pairs,),
        in_specs=[SCALAR]
        + [column_spec(a.shape[0], at * pairs // cols) for a, at in (q, k, v)],
        out_specs=[column_spec(rows, 0), log_spec(rows)],
        out_shape=[
            jax.ShapeDtypeStruct((rows, cols), BF),
            jax.ShapeDtypeStruct((pairs, 2, rows), F32),
        ],
        compiler_params=params_of(),
        cost_estimate=pl.CostEstimate(
            flops=4 * work, bytes_accessed=8 * rows * cols, transcendentals=work // HEAD_DIM
        ),
    )(limit, q[0], k[0], v[0])


def attend_back(limit, q, k, v, grad, logs, cols, causal):
    pairs = cols // (2 * HEAD_DIM)
    rows, count = q[0].shape[0], k[0].shape[0]
    work = rows * count * cols
    return pl.pallas_call(
        functools.partial(backward_kernel, causal),
        grid=(pairs,),
        in_specs=[SCALAR]
        + [column_spec(a.shape[0], at * pairs // cols) for a, at in (q, k, v)]
        + [column_spec(rows, 0), log_spec(rows)],
        out_specs=[column_spec(rows, 0), column_spec(count, 0), column_spec(count, 0)],
        out_shape=[jax.ShapeDtypeStruct((n, cols), BF) for n in (rows, count, count)],
        scratch_shapes=[pltpu.VMEM((count, 2 * HEAD_DIM), F32) for i in range(2)],
        compiler_params=params_of(),
        cost_estimate=pl.CostEstimate(
            flops=10 * work, bytes_accessed=16 * rows * cols, transcendentals=work // HEAD_DIM
        ),
    )(limit, q[0], k[0], v[0], grad, logs)


def row_spec(rows, cols):
    return pl.BlockSpec((rows, cols), lambda i: (i, 0))


def fixed_spec(*shape):
    return pl.BlockSpec(shape, lambda i: (0,) * len(shape))


CHUNK = 16


def fold(values):
    return values[: CHUNK // 2] + values[CHUNK // 2 :]


def chunked(step, visit, width, sum_ref=None):
    zero = jnp.zeros((CHUNK // 2, width), F32)
    gain, shift = zero, zero
    for start in range(0, step, CHUNK):
        terms = visit(slice(start, start + CHUNK))
        if sum_ref is not None:
            gain, shift = gain + fold(terms[0]), shift + fold(terms[1])
    if sum_ref is None:
        return
    sums = jnp.concatenate(
        [jnp.sum(gain, axis=0, keepdims=True), jnp.sum(shift, axis=0, keepdims=True)]
    )
    first = pl.program_id(0) == 0

    @pl.when(first)
    def _():
        sum_ref[...] = sums

    @pl.when(jnp.logical_not(first))
    def _():
        sum_ref[...] += sums


def norm_grad(hat, rstd, gain, grad):
    scaled = grad * gain
    first = jnp.mean(scaled, axis=-1, keepdims=True)
    second = jnp.mean(scaled * hat, axis=-1, keepdims=True)
    return rstd * (scaled - first - hat * second)


def norm_kernel(index, x_ref, own_ref, other_ref, p_ref, new_ref, out_ref):
    step, width = x_ref.shape
    gain, shift = p_ref[index : index + 1, :], p_ref[index + 4 : index + 5, :]

    def visit(at):
        x = x_ref[at, :].astype(F32) + own_ref[at, :].astype(F32) + other_ref[at, :].astype(F32)
        new_ref[at, :] = x
        hat, rstd = normalize(x)
        out_ref[at, :] = (hat * gain + shift).astype(BF)

    chunked(step, visit, width)


def norm_rows(index, x, own, other, params):
    rows, width = x.shape
    step = rows // 4
    row = row_spec(step, width)
    return pl.pallas_call(
        functools.partial(norm_kernel, index),
        grid=(4,),
        in_specs=[row, row, row, fixed_spec(*params.shape)],
        out_specs=[row, row],
        out_shape=[
            jax.ShapeDtypeStruct((rows, width), F32),
            jax.ShapeDtypeStruct((rows, width), BF),
        ],
        compiler_params=params_of(),
        cost_estimate=pl.CostEstimate(
            flops=20 * rows * width, bytes_accessed=14 * rows * width, transcendentals=rows
        ),
    )(x, own, other, params)


def last_kernel(
    limit_ref, x_ref, own_ref, other_ref, p_ref, cot_ref, out_ref, dx_ref, dy_ref, sum_ref
):
    step, width = x_ref.shape
    gain, shift = p_ref[3:4, :], p_ref[7:8, :]
    begin = pl.program_id(0) * step

    def visit(at):
        x = x_ref[at, :] + own_ref[at, :].astype(F32) + other_ref[at, :].astype(F32)
        hat, rstd = normalize(x)
        out_ref[at, :] = (hat * gain + shift).astype(BF)
        row = begin + at.start + lax.broadcasted_iota(jnp.int32, (CHUNK, 1), 0)
        grad = cot_ref[at, :].astype(F32) * (row < limit_ref[0]).astype(F32)
        dx = norm_grad(hat, rstd, gain, grad)
        dx_ref[at, :] = dx
        dy_ref[at, :] = dx.astype(BF)
        return grad * hat, grad

    chunked(step, visit, width, sum_ref)


def norm_last(limit, x, own, other, params, cot):
    rows, width = x.shape
    step = rows // 4
    row = row_spec(step, width)
    return pl.pallas_call(
        last_kernel,
        grid=(4,),
        in_specs=[SCALAR, row, row, row, fixed_spec(*params.shape), row],
        out_specs=[row, row, row, fixed_spec(2, width)],
        out_shape=[
            jax.ShapeDtypeStruct((rows, width), BF),
            jax.ShapeDtypeStruct((rows, width), F32),
            jax.ShapeDtypeStruct((rows, width), BF),
            jax.ShapeDtypeStruct((2, width), F32),
        ],
        compiler_params=params_of(),
        cost_estimate=pl.CostEstimate(
            flops=40 * rows * width, bytes_accessed=20 * rows * width, transcendentals=rows
        ),
    )(limit, x, own, other, params, cot)


def back_kernel(index, x_ref, own_ref, other_ref, dres_ref, p_ref, dx_ref, *refs):
    step, width = x_ref.shape
    gain = p_ref[index : index + 1, :]

    def visit(at):
        hat, rstd = normalize(x_ref[at, :].astype(F32))
        grad = own_ref[at, :].astype(F32) + other_ref[at, :].astype(F32)
        dx = dres_ref[at, :] + norm_grad(hat, rstd, gain, grad)
        dx_ref[at, :] = dx
        if index:
            refs[0][at, :] = dx.astype(BF)
        return grad * hat, grad

    chunked(step, visit, width, refs[-1])


def norm_rows_back(index, x, own, other, dres, params):
    rows, width = x.shape
    step = rows // 4
    row = row_spec(step, width)
    lower = 1 if index else 0
    return pl.pallas_call(
        functools.partial(back_kernel, index),
        grid=(4,),
        in_specs=[row, row, row, row, fixed_spec(*params.shape)],
        out_specs=[row] + [row] * lower + [fixed_spec(2, width)],
        out_shape=[jax.ShapeDtypeStruct((rows, width), F32)]
        + [jax.ShapeDtypeStruct((rows, width), BF)] * lower
        + [jax.ShapeDtypeStruct((2, width), F32)],
        compiler_params=params_of(),
        cost_estimate=pl.CostEstimate(
            flops=30 * rows * width, bytes_accessed=18 * rows * width, transcendentals=rows
        ),
    )(x, own, other, dres, params)


FFN_STEPS = 4


def place_kernel(place_ref, from_ref, up_ref, down_ref, sems):
    blocks = place_ref.shape[0]
    size = up_ref.shape[0] // blocks
    copies = []
    for half, to_ref in enumerate((up_ref, down_ref)):
        for label in range(blocks):
            at = pl.multiple_of(place_ref[label] * size, size)
            copy = pltpu.make_async_copy(
                from_ref.at[half, pl.ds(at, size), :],
                to_ref.at[pl.ds(label * size, size), :],
                sems.at[half, label],
            )
            copy.start()
            copies.append(copy)
    for copy in copies:
        copy.wait()


def placed_weights(place, ffn):
    parts, width, units = ffn.shape
    anywhere = pl.BlockSpec(memory_space=pl.ANY)
    return pl.pallas_call(
        place_kernel,
        in_specs=[SCALAR, anywhere],
        out_specs=[anywhere] * 2,
        out_shape=[jax.ShapeDtypeStruct((width, units), BF)] * 2,
        scratch_shapes=[pltpu.SemaphoreType.DMA((2, place.shape[0]))],
        compiler_params=pltpu.CompilerParams(vmem_limit_bytes=1024 * 1024),
        cost_estimate=pl.CostEstimate(
            flops=0, bytes_accessed=4 * parts * width * units, transcendentals=0
        ),
    )(place, ffn)


def outer_kernel(place_ref, x_ref, d_ref, out_ref, turned):
    @pl.when(pl.program_id(0) == 0)
    def _():
        turned[...] = x_ref[...].T

    full = mm(turned[...], d_ref[...]).astype(BF)
    blocks = place_ref.shape[0]
    size = full.shape[0] // blocks
    for label in range(blocks):
        at = pl.multiple_of(place_ref[label] * size, size)
        out_ref[pl.ds(at, size), :] = full[label * size : (label + 1) * size]


def outer(place, x, d):
    rows, width = x.shape
    units = d.shape[1]
    step = units // FFN_STEPS
    col = pl.BlockSpec((width, step), lambda i: (0, i))
    return pl.pallas_call(
        outer_kernel,
        grid=(FFN_STEPS,),
        in_specs=[SCALAR, fixed_spec(rows, width), pl.BlockSpec((rows, step), lambda i: (0, i))],
        out_specs=col,
        out_shape=jax.ShapeDtypeStruct((width, units), BF),
        scratch_shapes=[pltpu.VMEM((width, rows), BF)],
        compiler_params=params_of(),
        cost_estimate=pl.CostEstimate(
            flops=2 * rows * width * units,
            bytes_accessed=2 * width * units + 2 * rows * units,
            transcendentals=0,
        ),
    )(place, x, d)


def terms_kernel(order, lines, *refs):
    step = pl.program_id(0)
    count, blocks = len(set(order)), len(order)
    lefts, rights, refs = refs[:count], refs[count : count + blocks], refs[count + blocks :]
    turned = refs[-count:]
    for block in range(blocks):

        @pl.when(step == block)
        def _(block=block):
            at = order[block]
            if order.index(at) == block:
                turned[at][...] = lefts[at][...].T
            full = mm(turned[at][...], rights[block][...]).astype(BF)
            quarter = full.shape[0] // 4
            if lines:
                keep_ref, send_ref = refs[:2]
                half = quarter // 2
                for label in range(4):
                    middle = label * quarter + half
                    keep_ref[0, label] = full[middle - half : middle]
                    send_ref[0, label] = full[middle : middle + half]
            else:
                one_ref, two_ref, y_ref, x_ref, own_ref = refs[:5]
                own_ref[0] = full[:quarter]
                y_ref[0] = full[quarter : 2 * quarter]
                x_ref[0] = full[2 * quarter : 3 * quarter]
                (one_ref if block < blocks // 2 else two_ref)[0] = full[3 * quarter :]


def grad_terms(lefts, order, rights, lines=False):
    width, cols = lefts[0].shape[1], rights[0].shape[1]
    blocks = len(order)
    middle = blocks // 2
    quarter = width // 4
    same = lambda i: i
    if lines:
        spec = pl.BlockSpec((1, 4, quarter // 2, cols), lambda i: (i, 0, 0, 0))
        out_specs = [spec] * 2
        out_shape = [jax.ShapeDtypeStruct((blocks, 4, quarter // 2, cols), BF)] * 2
    else:
        piece = lambda place: pl.BlockSpec((1, quarter, cols), lambda i: (place(i), 0, 0))
        shape = lambda n: jax.ShapeDtypeStruct((n, quarter, cols), BF)
        out_specs = [
            piece(lambda i: jnp.minimum(i, middle - 1)),
            piece(lambda i: jnp.maximum(i - middle, 0)),
        ] + [piece(same)] * 3
        out_shape = [shape(middle)] * 2 + [shape(blocks)] * 3
    return pl.pallas_call(
        functools.partial(terms_kernel, order, lines),
        grid=(blocks,),
        in_specs=[fixed_spec(*v.shape) for v in (*lefts, *rights)],
        out_specs=out_specs,
        out_shape=out_shape,
        scratch_shapes=[pltpu.VMEM((width, v.shape[0]), BF) for v in lefts],
        compiler_params=params_of(),
        cost_estimate=pl.CostEstimate(
            flops=2 * blocks * lefts[0].shape[0] * width * cols,
            bytes_accessed=2 * blocks * width * cols + 16 * lefts[0].shape[0] * width,
            transcendentals=0,
        ),
    )(*lefts, *rights)


def behind(values, earlier):
    return lax.optimization_barrier((values, earlier))[0]


def make_body(n_dp):
    bits = n_dp.bit_length() - 1
    assert n_dp == 1 << bits

    def hop(values, bit):
        return lax.ppermute(values, "dp", [(i, i ^ (1 << bit)) for i in range(n_dp)])

    far = range(bits - 1, 1, -1)

    def gather_far(held, bits_now, after):
        for bit in bits_now:
            after = hop(behind(held, after), bit)
            held = jnp.stack([held, after])
        return held, after

    def inner_rows(v, start, stop):
        return lax.slice_in_dim(v, start, stop, axis=v.ndim - 2)

    def gather_sides(held, after):
        held = behind(held, after)
        return hop(held, 0), hop(held, 1)

    def gather_corner(by_x, by_y, cut, after):
        first = behind(inner_rows(by_y, 0, cut), after)
        second = behind(inner_rows(by_x, cut, by_x.shape[-2]), after)
        return hop(first, 0), hop(second, 1)

    def gathered(held, sides, corner, cut):
        (by_x, by_y), (first, second) = sides, corner

        def rows(start, stop):
            last, offset = (first, 0) if stop <= cut else (second, cut)
            parts = [inner_rows(v, start, stop) for v in (held, by_y, by_x)]
            parts.append(inner_rows(last, start - offset, stop - offset))
            return jnp.concatenate(
                [v.reshape(-1, stop - start, v.shape[-1]) for v in parts]
            )

        return rows

    def full_weight(rows, start, stop):
        return rows(start, stop).reshape(-1, rows(start, stop).shape[-1])

    def plus(v, w):
        return (v.astype(F32) + w.astype(F32)).astype(BF)

    def scatter_near(pieces, late):
        one, two, for_y, for_x, own = pieces
        middle = one.shape[0]
        got_one, got_two = behind((hop(one, 0), hop(two, 1)), late)
        for_y = for_y.at[:middle].set(plus(for_y[:middle], got_one))
        for_x = for_x.at[middle:].set(plus(for_x[middle:], got_two))
        got_x, got_y = hop(for_x, 0), hop(for_y, 1)
        return own, (for_x, for_y), (got_x, got_y)

    def near_total(own, got):
        return own.astype(F32) + got[0].astype(F32) + got[1].astype(F32)

    def scatter_far(held):
        parts, feats, cols = held.shape
        held = held.reshape(parts, -1, feats * 4 // n_dp, cols)
        for count, bit in enumerate(reversed(far)):
            middle = held.shape[1] // 2
            held = held[:, :middle].astype(F32) + hop(held[:, middle:], bit).astype(F32)
            if count < len(far) - 1:
                held = held.astype(BF)
        return held[:, 0]

    def lines_first(keep, send):
        for count, bit in enumerate(reversed(far)):
            if count:
                middle = keep.shape[2] // 2
                keep, send = keep[:, :, :middle], keep[:, :, middle:]
            keep = plus(keep, hop(send, bit))
        middle = keep.shape[0] // 2
        return keep[:middle, 3], keep[middle:, 3], keep[:, 1], keep[:, 2], keep[:, 0]

    planes = [[4 * z + p for p in range(4)] for z in range(n_dp // 4)]
    lines = [[4 * z + p for z in range(n_dp // 4)] for p in range(4)]
    plane_first = [chip for line in lines for chip in line]

    def sum_plane(full):
        return lax.psum_scatter(
            full, "dp", scatter_dimension=0, tiled=True, axis_index_groups=planes
        )

    def sum_lines(full):
        return lax.psum_scatter(
            full, "dp", scatter_dimension=0, tiled=True, axis_index_groups=lines
        )

    def line_hops(full):
        rows, cols = full.shape
        held = full.reshape((2,) * len(far) + (rows * 4 // n_dp, cols))
        for count, bit in enumerate(reversed(far)):
            mine = (lax.axis_index("dp") >> bit) & 1
            axis = held.ndim - 3
            keep = lax.dynamic_index_in_dim(held, mine, axis, keepdims=False)
            send = lax.dynamic_index_in_dim(held, 1 - mine, axis, keepdims=False)
            held = keep.astype(F32) + hop(send.astype(BF), bit).astype(F32)
        return held

    def scatter_small(full, late):
        lead, feats = full.shape
        held = full.reshape((lead,) + (2,) * bits + (feats // n_dp,))
        for bit in reversed(far):
            keep = lax.index_in_dim(held, 0, 3, keepdims=False)
            held = keep + hop(lax.index_in_dim(held, 1, 3, keepdims=False), bit)
        held = behind(held, late)
        for bit in (0, 1):
            keep = lax.index_in_dim(held, 0, 1, keepdims=False)
            held = keep + hop(lax.index_in_dim(held, 1, 1, keepdims=False), bit)
        return held

    def body(
        tokens,
        enc_states,
        utt_lengths,
        enc_lengths,
        self_qkv,
        self_out,
        cross_qkv,
        cross_out,
        ffn_proj,
        norm_gains,
        norm_biases,
        cotangent,
    ):
        width = tokens.shape[1]
        feats = norm_gains.shape[1]
        core = lax.axis_index("tensor")
        me = lax.axis_index("dp")

        block = width // n_dp
        cols = jnp.arange(width, dtype=jnp.int32)
        labels = cols // block
        reverse = jnp.zeros_like(labels)
        for bit in range(bits):
            reverse = reverse | (((labels >> (bits - 1 - bit)) & 1) << bit)
        source = (me ^ reverse) * block + cols % block
        relabel = (cols[:, None] == source[None, :]).astype(BF)
        chip = source // block
        placed = ((chip & 3) * (n_dp // 4) + (chip >> 2)) * block + cols % block
        place = placed[::block] // block
        replace = (placed[:, None] == cols[None, :]).astype(BF)
        direct = feats % 16 == 0

        beside = lambda *v: jnp.concatenate(v, axis=-1)
        above = lambda *v: jnp.concatenate(v)
        params = jnp.concatenate([norm_gains, norm_biases]).reshape(1, 8 * feats)
        params = jnp.pad(params, ((0, 7), (0, 2 * self_out.shape[1] - 8 * feats)))
        ffn = lax.all_gather(
            ffn_proj, "dp", axis=1, tiled=True, axis_index_groups=[plane_first]
        )
        if direct:
            up, down = placed_weights(place, ffn)
        else:
            up, down = [mm(replace, ffn[i]).astype(BF) for i in (0, 1)]
            place = jnp.zeros((1,), jnp.int32)
        s_a = above(beside(self_qkv[0], self_qkv[1]), beside(self_qkv[2], self_out), params)
        s_c = above(beside(cross_qkv[1], cross_qkv[2]), beside(cross_qkv[0], cross_out))
        held_a, token = gather_far(s_a, far, norm_gains)
        sides_a = gather_sides(held_a, token)
        held_c, token = gather_far(s_c, far, token)
        corner_a = gather_corner(*sides_a, feats, sides_a)
        sides_c = gather_sides(held_c, sides_a)
        corner_c = gather_corner(*sides_c, feats, sides_c)
        weights = [
            gathered(held_a, sides_a, corner_a, feats),
            gathered(held_c, sides_c, corner_c, feats),
        ]
        w_qk, w_vo = full_weight(weights[0], 0, feats), full_weight(weights[0], feats, 2 * feats)
        params = weights[0](2 * feats, 2 * feats + 8)[:, 0, : 8 * feats]
        params = params.reshape(n_dp, 8, feats).transpose(1, 0, 2).reshape(8, width).astype(F32)
        c_kv, c_qo = [full_weight(weights[1], i * feats, (i + 1) * feats) for i in (0, 1)]
        inner_cols = self_out.shape[1]
        w_v, w_o = w_vo[:, :inner_cols], w_vo[:, inner_cols:]
        c_q, c_o = c_qo[:, :inner_cols], c_qo[:, inner_cols:]

        def whole(mine):
            other = swap(mine)
            return jnp.where(
                core == 0,
                jnp.concatenate([mine, other]),
                jnp.concatenate([other, mine]),
            )

        def relabeled(values):
            return mm(values, relabel).astype(BF)

        def own(values):
            size = values.shape[0] // 2
            return lax.dynamic_slice_in_dim(values, core * size, size)

        def other(values):
            size = values.shape[0] // 2
            return lax.dynamic_slice_in_dim(values, (1 - core) * size, size)

        def restored(values):
            high = values.astype(BF)
            low = (values - high.astype(F32)).astype(BF)
            return mm_t(high, relabel) + mm_t(low, relabel)

        x0 = whole(relabeled(tokens))
        enc = whole(relabeled(enc_states))
        cot = whole(relabeled(cotangent))

        hat0, rstd0 = normalize(x0.astype(F32))
        normed1 = (hat0 * params[0] + params[4]).astype(BF)
        qk1 = mm(normed1, w_qk).astype(BF)
        v1 = mm(normed1, w_v).astype(BF)
        first = (qk1, 0), (qk1, inner_cols), (v1, 0)
        o1, logs1 = attend(utt_lengths, *first, inner_cols, True)
        y1 = mm_t(o1, w_o).astype(BF)
        x1, normed2 = norm_rows(1, x0, y1, swap(y1), params)
        kv2 = mm(enc, c_kv).astype(BF)
        q2 = mm(normed2, c_q).astype(BF)
        second = (q2, 0), (kv2, 0), (kv2, inner_cols)
        q2, up, down = lax.optimization_barrier((q2, up, down))
        second = (q2, 0), (kv2, 0), (kv2, inner_cols)
        o2, logs2 = attend(enc_lengths, *second, inner_cols, False)
        y2 = mm_t(o2, c_o).astype(BF)
        x2, normed3 = norm_rows(2, x1, y2, swap(y2), params)
        act, slope = gelu_both(mm(normed3, up))
        act, slope = lax.optimization_barrier((act.astype(BF), slope.astype(BF)))
        y3 = mm_t(act, down).astype(BF)
        out, dx3, dy3, sums3 = norm_last(utt_lengths, x2, y3, swap(y3), params, cot)

        def for_planes(x, d):
            full = outer(place, x, d)
            return full if direct else t_mm(replace, full).astype(BF)

        d_down = for_planes(dy3, act)
        s_down = sum_plane(d_down)
        du = (mm(behind(dy3, d_down), down) * slope.astype(F32)).astype(BF)
        n3 = mm_t(du, up).astype(BF)
        s_up = sum_plane(for_planes(normed3, du))
        dx2, dy2, sums2 = norm_rows_back(2, x2, n3, swap(n3), dx3, params)
        do2 = mm(dy2, c_o).astype(BF)
        dq2, dk2, dv2 = attend_back(
            enc_lengths, *second, do2, logs2, inner_cols, False
        )
        terms_c = grad_terms((enc, normed2, dy2), (0, 0, 1, 2), (dk2, dv2, dq2, o2))
        n2 = mm_t(dq2, c_q).astype(BF)
        dx1, dy1, sums1 = norm_rows_back(1, x1, n2, swap(n2), dx2, params)
        do1 = mm(dy1, w_o).astype(BF)
        dq1, dk1, dv1 = attend_back(
            utt_lengths, *first, do1, logs1, inner_cols, True
        )
        own_c, sent_c, got_c = scatter_near(terms_c, do1)
        terms_qk = grad_terms((normed1,), (0, 0), (dq1, dk1))
        terms_vo = grad_terms((normed1, dy1), (0, 1), (dv1, o1), True)
        n1 = (mm_t(beside(dq1, dk1), w_qk) + mm_t(dv1, w_v)).astype(BF)
        dx0, sums0 = norm_rows_back(0, x0, n1, swap(n1), dx1, params)
        token_grad = restored(own(dx0))
        output = mm_t(own(out), relabel).astype(BF)
        enc_part = mm_t(dk2, c_kv[:, :inner_cols]) + mm_t(dv2, c_kv[:, inner_cols:])
        enc_grad = restored(own(enc_part) + swap(other(enc_part).astype(BF)).astype(F32))

        s_down = line_hops(s_down)
        own_qk, sent_qk, got_qk = scatter_near(terms_qk, dx0)
        s_up = sum_lines(behind(s_up, sent_qk))
        s_cross = scatter_far(near_total(own_c, got_c).astype(BF))
        s_vo, sent_vo, got_vo = scatter_near(lines_first(*terms_vo), sent_qk)
        s_vo = near_total(s_vo, got_vo)
        s_qk = scatter_far(near_total(own_qk, got_qk).astype(BF))
        sums = (sums0, sums1, sums2, sums3)
        terms = jnp.concatenate([v[:1] for v in sums] + [v[1:] for v in sums])
        terms = scatter_small(terms, got_qk)
        part = terms.shape[1] // 2
        terms = lax.dynamic_slice_in_dim(terms, core * part, part, axis=1)
        return (
            output,
            token_grad,
            enc_grad,
            jnp.concatenate([s_qk, s_vo[:1]]),
            s_vo[1],
            jnp.concatenate([s_cross[2:3], s_cross[:2]]),
            s_cross[3],
            jnp.stack([s_up.astype(F32), s_down]),
            terms[:4],
            terms[4:],
        )

    return body


def solution(mesh):
    return jax.shard_map(
        make_body(mesh.shape["dp"]),
        mesh=mesh,
        in_specs=(
            P(("dp", "tensor"), None),
            P(("dp", "tensor"), None),
            P("dp"),
            P("dp"),
            P(None, "dp", "tensor"),
            P("dp", "tensor"),
            P(None, "dp", "tensor"),
            P("dp", "tensor"),
            P(None, "dp", "tensor"),
            P(None, "dp"),
            P(None, "dp"),
            P(("dp", "tensor"), None),
        ),
        out_specs=(
            P(("dp", "tensor"), None),
            P(("dp", "tensor"), None),
            P(("dp", "tensor"), None),
            P(None, "dp", "tensor"),
            P("dp", "tensor"),
            P(None, "dp", "tensor"),
            P("dp", "tensor"),
            P(None, "dp", "tensor"),
            P(None, ("dp", "tensor")),
            P(None, ("dp", "tensor")),
        ),
        check_vma=False,
    )
```

```python
import functools

import jax
import jax.numpy as jnp
from jax import lax
from jax.experimental import pallas as pl
from jax.experimental.pallas import tpu as pltpu
from jax.sharding import PartitionSpec as P

HEAD_DIM = 64
EPSILON = 1e-05
NEG_FILL = -1000000000.0
BF = jnp.bfloat16
F32 = jnp.float32


def dot(a, b, dims):
    return lax.dot_general(a, b, (dims, ((), ())), preferred_element_type=F32)


def mm(a, b):
    return dot(a, b, ((1,), (0,)))


def mm_t(a, b):
    return dot(a, b, ((1,), (1,)))


def t_mm(a, b):
    return dot(a, b, ((0,), (0,)))


def swap(values):
    return lax.ppermute(values, "tensor", [(0, 1), (1, 0)])


def normalize(values):
    centre = jnp.mean(values, axis=-1, keepdims=True)
    centred = values - centre
    spread = jnp.mean(centred * centred, axis=-1, keepdims=True)
    rstd = lax.rsqrt(spread + EPSILON)
    return centred * rstd, rstd


def gelu_both(z):
    c = 0.7978845608028654
    square = z * z
    t = jnp.tanh(z * (c + 0.044715 * c * square))
    gate = 0.5 + 0.5 * t
    value = z * gate
    return value, gate + value * (1.0 - t) * (c + 3.0 * 0.044715 * c * square)


def masked(values, head):
    lane = lax.broadcasted_iota(jnp.int32, values.shape, 1)
    return jnp.where((lane < HEAD_DIM) == (head == 0), values, jnp.zeros_like(values))


def scores_of(keys, queries, start, limit, causal):
    raw = mm_t(keys, queries)
    key = lax.broadcasted_iota(jnp.int32, raw.shape, 0)
    allowed = key < limit
    if causal:
        query = start + lax.broadcasted_iota(jnp.int32, raw.shape, 1)
        allowed = allowed & (key <= query)
    return jnp.where(allowed, raw, NEG_FILL)


def blocks_of(rows, count, causal):
    if causal:
        half = rows // 2
        return [(0, half, half), (half, half, count)]
    return [(0, rows, count)]


def forward_kernel(causal, limit_ref, q_ref, k_ref, v_ref, out_ref, log_ref):
    limit = limit_ref[0]
    scale = HEAD_DIM ** (-0.5)
    for start, size, reach in blocks_of(q_ref.shape[0], k_ref.shape[0], causal):
        queries = (q_ref[start : start + size, :].astype(F32) * scale).astype(BF)
        mixed = None
        for head in range(2):
            keys = masked(k_ref[:reach, :], head)
            values = masked(v_ref[:reach, :], head)
            scores = scores_of(keys, queries, start, limit, causal)
            top = jnp.max(scores, axis=0, keepdims=True)
            exps = jnp.exp(scores - top)
            total = jnp.sum(exps, axis=0, keepdims=True)
            probs = (exps * (1.0 / total)).astype(BF)
            part = t_mm(probs, values)
            mixed = part if mixed is None else mixed + part
            log_ref[0, head : head + 1, start : start + size] = top + jnp.log(total)
        out_ref[start : start + size, :] = mixed.astype(BF)


def backward_kernel(
    causal, limit_ref, q_ref, k_ref, v_ref, do_ref, log_ref, dq_ref, dk_ref, dv_ref, sk, sv
):
    limit = limit_ref[0]
    scale = HEAD_DIM ** (-0.5)
    sk[...] = jnp.zeros_like(sk)
    sv[...] = jnp.zeros_like(sv)
    for start, size, reach in blocks_of(q_ref.shape[0], k_ref.shape[0], causal):
        queries = (q_ref[start : start + size, :].astype(F32) * scale).astype(BF)
        grad = do_ref[start : start + size, :]
        total = None
        for head in range(2):
            keys = masked(k_ref[:reach, :], head)
            values = masked(v_ref[:reach, :], head)
            scores = scores_of(keys, queries, start, limit, causal)
            probs = jnp.exp(scores - log_ref[0, head : head + 1, start : start + size])
            sv[:reach, :] += mm(probs.astype(BF), masked(grad, head))
            dprobs = mm_t(values, grad)
            inner = jnp.sum(dprobs * probs, axis=0, keepdims=True)
            ds = (probs * (dprobs - inner)).astype(BF)
            sk[:reach, :] += mm(ds, masked(queries, head))
            part = t_mm(ds, keys)
            total = part if total is None else total + part
        dq_ref[start : start + size, :] = (total * scale).astype(BF)
    dk_ref[...] = sk[...].astype(BF)
    dv_ref[...] = sv[...].astype(BF)


VMEM_LIMIT = 16 * 1024 * 1024


def params_of():
    return pltpu.CompilerParams(
        dimension_semantics=("arbitrary",), vmem_limit_bytes=VMEM_LIMIT
    )


def column_spec(rows, offset):
    return pl.BlockSpec((rows, 2 * HEAD_DIM), lambda i: (0, i + offset))


def log_spec(rows):
    return pl.BlockSpec((1, 2, rows), lambda i: (i, 0, 0))


SCALAR = pl.BlockSpec(memory_space=pltpu.SMEM)


def attend(limit, q, k, v, cols, causal):
    pairs = cols // (2 * HEAD_DIM)
    rows, count = q[0].shape[0], k[0].shape[0]
    work = rows * count * cols
    return pl.pallas_call(
        functools.partial(forward_kernel, causal),
        grid=(pairs,),
        in_specs=[SCALAR]
        + [column_spec(a.shape[0], at * pairs // cols) for a, at in (q, k, v)],
        out_specs=[column_spec(rows, 0), log_spec(rows)],
        out_shape=[
            jax.ShapeDtypeStruct((rows, cols), BF),
            jax.ShapeDtypeStruct((pairs, 2, rows), F32),
        ],
        compiler_params=params_of(),
        cost_estimate=pl.CostEstimate(
            flops=4 * work, bytes_accessed=8 * rows * cols, transcendentals=work // HEAD_DIM
        ),
    )(limit, q[0], k[0], v[0])


def attend_back(limit, q, k, v, grad, logs, cols, causal):
    pairs = cols // (2 * HEAD_DIM)
    rows, count = q[0].shape[0], k[0].shape[0]
    work = rows * count * cols
    return pl.pallas_call(
        functools.partial(backward_kernel, causal),
        grid=(pairs,),
        in_specs=[SCALAR]
        + [column_spec(a.shape[0], at * pairs // cols) for a, at in (q, k, v)]
        + [column_spec(rows, 0), log_spec(rows)],
        out_specs=[column_spec(rows, 0), column_spec(count, 0), column_spec(count, 0)],
        out_shape=[jax.ShapeDtypeStruct((n, cols), BF) for n in (rows, count, count)],
        scratch_shapes=[pltpu.VMEM((count, 2 * HEAD_DIM), F32) for i in range(2)],
        compiler_params=params_of(),
        cost_estimate=pl.CostEstimate(
            flops=10 * work, bytes_accessed=16 * rows * cols, transcendentals=work // HEAD_DIM
        ),
    )(limit, q[0], k[0], v[0], grad, logs)


def row_spec(rows, cols):
    return pl.BlockSpec((rows, cols), lambda i: (i, 0))


def fixed_spec(*shape):
    return pl.BlockSpec(shape, lambda i: (0,) * len(shape))


CHUNK = 16


def fold(values):
    return values[: CHUNK // 2] + values[CHUNK // 2 :]


def chunked(step, visit, width, sum_ref=None):
    zero = jnp.zeros((CHUNK // 2, width), F32)
    gain, shift = zero, zero
    for start in range(0, step, CHUNK):
        terms = visit(slice(start, start + CHUNK))
        if sum_ref is not None:
            gain, shift = gain + fold(terms[0]), shift + fold(terms[1])
    if sum_ref is None:
        return
    sums = jnp.concatenate(
        [jnp.sum(gain, axis=0, keepdims=True), jnp.sum(shift, axis=0, keepdims=True)]
    )
    first = pl.program_id(0) == 0

    @pl.when(first)
    def _():
        sum_ref[...] = sums

    @pl.when(jnp.logical_not(first))
    def _():
        sum_ref[...] += sums


def norm_grad(hat, rstd, gain, grad):
    scaled = grad * gain
    first = jnp.mean(scaled, axis=-1, keepdims=True)
    second = jnp.mean(scaled * hat, axis=-1, keepdims=True)
    return rstd * (scaled - first - hat * second)


def norm_kernel(index, x_ref, own_ref, other_ref, p_ref, new_ref, out_ref):
    step, width = x_ref.shape
    gain, shift = p_ref[index : index + 1, :], p_ref[index + 4 : index + 5, :]

    def visit(at):
        x = x_ref[at, :].astype(F32) + own_ref[at, :].astype(F32) + other_ref[at, :].astype(F32)
        new_ref[at, :] = x
        hat, rstd = normalize(x)
        out_ref[at, :] = (hat * gain + shift).astype(BF)

    chunked(step, visit, width)


def norm_rows(index, x, own, other, params):
    rows, width = x.shape
    step = rows // 4
    row = row_spec(step, width)
    return pl.pallas_call(
        functools.partial(norm_kernel, index),
        grid=(4,),
        in_specs=[row, row, row, fixed_spec(*params.shape)],
        out_specs=[row, row],
        out_shape=[
            jax.ShapeDtypeStruct((rows, width), F32),
            jax.ShapeDtypeStruct((rows, width), BF),
        ],
        compiler_params=params_of(),
        cost_estimate=pl.CostEstimate(
            flops=20 * rows * width, bytes_accessed=14 * rows * width, transcendentals=rows
        ),
    )(x, own, other, params)


def last_kernel(
    limit_ref, x_ref, own_ref, other_ref, p_ref, cot_ref, out_ref, dx_ref, dy_ref, sum_ref
):
    step, width = x_ref.shape
    gain, shift = p_ref[3:4, :], p_ref[7:8, :]
    begin = pl.program_id(0) * step

    def visit(at):
        x = x_ref[at, :] + own_ref[at, :].astype(F32) + other_ref[at, :].astype(F32)
        hat, rstd = normalize(x)
        out_ref[at, :] = (hat * gain + shift).astype(BF)
        row = begin + at.start + lax.broadcasted_iota(jnp.int32, (CHUNK, 1), 0)
        grad = cot_ref[at, :].astype(F32) * (row < limit_ref[0]).astype(F32)
        dx = norm_grad(hat, rstd, gain, grad)
        dx_ref[at, :] = dx
        dy_ref[at, :] = dx.astype(BF)
        return grad * hat, grad

    chunked(step, visit, width, sum_ref)


def norm_last(limit, x, own, other, params, cot):
    rows, width = x.shape
    step = rows // 4
    row = row_spec(step, width)
    return pl.pallas_call(
        last_kernel,
        grid=(4,),
        in_specs=[SCALAR, row, row, row, fixed_spec(*params.shape), row],
        out_specs=[row, row, row, fixed_spec(2, width)],
        out_shape=[
            jax.ShapeDtypeStruct((rows, width), BF),
            jax.ShapeDtypeStruct((rows, width), F32),
            jax.ShapeDtypeStruct((rows, width), BF),
            jax.ShapeDtypeStruct((2, width), F32),
        ],
        compiler_params=params_of(),
        cost_estimate=pl.CostEstimate(
            flops=40 * rows * width, bytes_accessed=20 * rows * width, transcendentals=rows
        ),
    )(limit, x, own, other, params, cot)


def back_kernel(index, x_ref, own_ref, other_ref, dres_ref, p_ref, dx_ref, *refs):
    step, width = x_ref.shape
    gain = p_ref[index : index + 1, :]

    def visit(at):
        hat, rstd = normalize(x_ref[at, :].astype(F32))
        grad = own_ref[at, :].astype(F32) + other_ref[at, :].astype(F32)
        dx = dres_ref[at, :] + norm_grad(hat, rstd, gain, grad)
        dx_ref[at, :] = dx
        if index:
            refs[0][at, :] = dx.astype(BF)
        return grad * hat, grad

    chunked(step, visit, width, refs[-1])


def norm_rows_back(index, x, own, other, dres, params):
    rows, width = x.shape
    step = rows // 4
    row = row_spec(step, width)
    lower = 1 if index else 0
    return pl.pallas_call(
        functools.partial(back_kernel, index),
        grid=(4,),
        in_specs=[row, row, row, row, fixed_spec(*params.shape)],
        out_specs=[row] + [row] * lower + [fixed_spec(2, width)],
        out_shape=[jax.ShapeDtypeStruct((rows, width), F32)]
        + [jax.ShapeDtypeStruct((rows, width), BF)] * lower
        + [jax.ShapeDtypeStruct((2, width), F32)],
        compiler_params=params_of(),
        cost_estimate=pl.CostEstimate(
            flops=30 * rows * width, bytes_accessed=18 * rows * width, transcendentals=rows
        ),
    )(x, own, other, dres, params)


FFN_STEPS = 4


def place_kernel(place_ref, from_ref, up_ref, down_ref, sems):
    blocks = place_ref.shape[0]
    size = up_ref.shape[0] // blocks
    copies = []
    for half, to_ref in enumerate((up_ref, down_ref)):
        for label in range(blocks):
            at = pl.multiple_of(place_ref[label] * size, size)
            copy = pltpu.make_async_copy(
                from_ref.at[half, pl.ds(at, size), :],
                to_ref.at[pl.ds(label * size, size), :],
                sems.at[half, label],
            )
            copy.start()
            copies.append(copy)
    for copy in copies:
        copy.wait()


def placed_weights(place, ffn):
    parts, width, units = ffn.shape
    anywhere = pl.BlockSpec(memory_space=pl.ANY)
    return pl.pallas_call(
        place_kernel,
        in_specs=[SCALAR, pl.BlockSpec(memory_space=pltpu.HBM)],
        out_specs=[anywhere] * 2,
        out_shape=[jax.ShapeDtypeStruct((width, units), BF)] * 2,
        scratch_shapes=[pltpu.SemaphoreType.DMA((2, place.shape[0]))],
        compiler_params=pltpu.CompilerParams(vmem_limit_bytes=1024 * 1024),
        cost_estimate=pl.CostEstimate(
            flops=0, bytes_accessed=4 * parts * width * units, transcendentals=0
        ),
    )(place, ffn)


def outer_kernel(place_ref, x_ref, d_ref, out_ref, turned):
    @pl.when(pl.program_id(0) == 0)
    def _():
        turned[...] = x_ref[...].T

    full = mm(turned[...], d_ref[...]).astype(BF)
    blocks = place_ref.shape[0]
    size = full.shape[0] // blocks
    for label in range(blocks):
        at = pl.multiple_of(place_ref[label] * size, size)
        out_ref[pl.ds(at, size), :] = full[label * size : (label + 1) * size]


def outer(place, x, d):
    rows, width = x.shape
    units = d.shape[1]
    step = units // FFN_STEPS
    col = pl.BlockSpec((width, step), lambda i: (0, i))
    return pl.pallas_call(
        outer_kernel,
        grid=(FFN_STEPS,),
        in_specs=[SCALAR, fixed_spec(rows, width), pl.BlockSpec((rows, step), lambda i: (0, i))],
        out_specs=col,
        out_shape=pltpu.HBM((width, units), BF),
        scratch_shapes=[pltpu.VMEM((width, rows), BF)],
        compiler_params=params_of(),
        cost_estimate=pl.CostEstimate(
            flops=2 * rows * width * units,
            bytes_accessed=2 * width * units + 2 * rows * units,
            transcendentals=0,
        ),
    )(place, x, d)


def terms_kernel(order, lines, *refs):
    step = pl.program_id(0)
    count, blocks = len(set(order)), len(order)
    lefts, rights, refs = refs[:count], refs[count : count + blocks], refs[count + blocks :]
    turned = refs[-count:]
    for block in range(blocks):

        @pl.when(step == block)
        def _(block=block):
            at = order[block]
            if order.index(at) == block:
                turned[at][...] = lefts[at][...].T
            full = mm(turned[at][...], rights[block][...]).astype(BF)
            quarter = full.shape[0] // 4
            if lines:
                keep_ref, send_ref = refs[:2]
                half = quarter // 2
                for label in range(4):
                    middle = label * quarter + half
                    keep_ref[0, label] = full[middle - half : middle]
                    send_ref[0, label] = full[middle : middle + half]
            else:
                one_ref, two_ref, y_ref, x_ref, own_ref = refs[:5]
                own_ref[0] = full[:quarter]
                y_ref[0] = full[quarter : 2 * quarter]
                x_ref[0] = full[2 * quarter : 3 * quarter]
                (one_ref if block < blocks // 2 else two_ref)[0] = full[3 * quarter :]


def grad_terms(lefts, order, rights, lines=False):
    width, cols = lefts[0].shape[1], rights[0].shape[1]
    blocks = len(order)
    middle = blocks // 2
    quarter = width // 4
    same = lambda i: i
    if lines:
        spec = pl.BlockSpec((1, 4, quarter // 2, cols), lambda i: (i, 0, 0, 0))
        out_specs = [spec] * 2
        out_shape = [jax.ShapeDtypeStruct((blocks, 4, quarter // 2, cols), BF)] * 2
    else:
        piece = lambda place: pl.BlockSpec((1, quarter, cols), lambda i: (place(i), 0, 0))
        shape = lambda n: jax.ShapeDtypeStruct((n, quarter, cols), BF)
        out_specs = [
            piece(lambda i: jnp.minimum(i, middle - 1)),
            piece(lambda i: jnp.maximum(i - middle, 0)),
        ] + [piece(same)] * 3
        out_shape = [shape(middle)] * 2 + [shape(blocks)] * 3
    return pl.pallas_call(
        functools.partial(terms_kernel, order, lines),
        grid=(blocks,),
        in_specs=[fixed_spec(*v.shape) for v in (*lefts, *rights)],
        out_specs=out_specs,
        out_shape=out_shape,
        scratch_shapes=[pltpu.VMEM((width, v.shape[0]), BF) for v in lefts],
        compiler_params=params_of(),
        cost_estimate=pl.CostEstimate(
            flops=2 * blocks * lefts[0].shape[0] * width * cols,
            bytes_accessed=2 * blocks * width * cols + 16 * lefts[0].shape[0] * width,
            transcendentals=0,
        ),
    )(*lefts, *rights)


def behind(values, earlier):
    return lax.optimization_barrier((values, earlier))[0]


def make_body(n_dp):
    bits = n_dp.bit_length() - 1
    assert n_dp == 1 << bits

    def hop(values, bit):
        return lax.ppermute(values, "dp", [(i, i ^ (1 << bit)) for i in range(n_dp)])

    far = range(bits - 1, 1, -1)

    def gather_far(held, bits_now, after):
        for bit in bits_now:
            after = hop(behind(held, after), bit)
            held = jnp.stack([held, after])
        return held, after

    def inner_rows(v, start, stop):
        return lax.slice_in_dim(v, start, stop, axis=v.ndim - 2)

    def gather_sides(held, after):
        held = behind(held, after)
        return hop(held, 0), hop(held, 1)

    def gather_corner(by_x, by_y, cut, after):
        first = behind(inner_rows(by_y, 0, cut), after)
        second = behind(inner_rows(by_x, cut, by_x.shape[-2]), after)
        return hop(first, 0), hop(second, 1)

    def gathered(held, sides, corner, cut):
        (by_x, by_y), (first, second) = sides, corner

        def rows(start, stop):
            last, offset = (first, 0) if stop <= cut else (second, cut)
            parts = [inner_rows(v, start, stop) for v in (held, by_y, by_x)]
            parts.append(inner_rows(last, start - offset, stop - offset))
            return jnp.concatenate(
                [v.reshape(-1, stop - start, v.shape[-1]) for v in parts]
            )

        return rows

    def full_weight(rows, start, stop):
        return rows(start, stop).reshape(-1, rows(start, stop).shape[-1])

    def plus(v, w):
        return (v.astype(F32) + w.astype(F32)).astype(BF)

    def scatter_near(pieces, late):
        one, two, for_y, for_x, own = pieces
        middle = one.shape[0]
        got_one, got_two = behind((hop(one, 0), hop(two, 1)), late)
        for_y = for_y.at[:middle].set(plus(for_y[:middle], got_one))
        for_x = for_x.at[middle:].set(plus(for_x[middle:], got_two))
        got_x, got_y = hop(for_x, 0), hop(for_y, 1)
        return own, (for_x, for_y), (got_x, got_y)

    def near_total(own, got):
        return own.astype(F32) + got[0].astype(F32) + got[1].astype(F32)

    def scatter_far(held):
        parts, feats, cols = held.shape
        held = held.reshape(parts, -1, feats * 4 // n_dp, cols)
        for count, bit in enumerate(reversed(far)):
            middle = held.shape[1] // 2
            held = held[:, :middle].astype(F32) + hop(held[:, middle:], bit).astype(F32)
            if count < len(far) - 1:
                held = held.astype(BF)
        return held[:, 0]

    def lines_first(keep, send):
        for count, bit in enumerate(reversed(far)):
            if count:
                middle = keep.shape[2] // 2
                keep, send = keep[:, :, :middle], keep[:, :, middle:]
            keep = plus(keep, hop(send, bit))
        middle = keep.shape[0] // 2
        return keep[:middle, 3], keep[middle:, 3], keep[:, 1], keep[:, 2], keep[:, 0]

    planes = [[4 * z + p for p in range(4)] for z in range(n_dp // 4)]
    lines = [[4 * z + p for z in range(n_dp // 4)] for p in range(4)]
    plane_first = [chip for line in lines for chip in line]

    def sum_plane(full):
        return lax.psum_scatter(
            full, "dp", scatter_dimension=0, tiled=True, axis_index_groups=planes
        )

    def sum_lines(full):
        return lax.psum_scatter(
            full, "dp", scatter_dimension=0, tiled=True, axis_index_groups=lines
        )

    def line_hops(full):
        rows, cols = full.shape
        held = full.reshape((2,) * len(far) + (rows * 4 // n_dp, cols))
        for count, bit in enumerate(reversed(far)):
            mine = (lax.axis_index("dp") >> bit) & 1
            axis = held.ndim - 3
            keep = lax.dynamic_index_in_dim(held, mine, axis, keepdims=False)
            send = lax.dynamic_index_in_dim(held, 1 - mine, axis, keepdims=False)
            held = keep.astype(F32) + hop(send.astype(BF), bit).astype(F32)
        return held

    def scatter_small(full, late):
        lead, feats = full.shape
        held = full.reshape((lead,) + (2,) * bits + (feats // n_dp,))
        for bit in reversed(far):
            keep = lax.index_in_dim(held, 0, 3, keepdims=False)
            held = keep + hop(lax.index_in_dim(held, 1, 3, keepdims=False), bit)
        held = behind(held, late)
        for bit in (0, 1):
            keep = lax.index_in_dim(held, 0, 1, keepdims=False)
            held = keep + hop(lax.index_in_dim(held, 1, 1, keepdims=False), bit)
        return held

    def body(
        tokens,
        enc_states,
        utt_lengths,
        enc_lengths,
        self_qkv,
        self_out,
        cross_qkv,
        cross_out,
        ffn_proj,
        norm_gains,
        norm_biases,
        cotangent,
    ):
        width = tokens.shape[1]
        feats = norm_gains.shape[1]
        core = lax.axis_index("tensor")
        me = lax.axis_index("dp")

        block = width // n_dp
        cols = jnp.arange(width, dtype=jnp.int32)
        labels = cols // block
        reverse = jnp.zeros_like(labels)
        for bit in range(bits):
            reverse = reverse | (((labels >> (bits - 1 - bit)) & 1) << bit)
        source = (me ^ reverse) * block + cols % block
        relabel = (cols[:, None] == source[None, :]).astype(BF)
        chip = source // block
        placed = ((chip & 3) * (n_dp // 4) + (chip >> 2)) * block + cols % block
        place = placed[::block] // block
        replace = (placed[:, None] == cols[None, :]).astype(BF)
        direct = feats % 16 == 0

        beside = lambda *v: jnp.concatenate(v, axis=-1)
        above = lambda *v: jnp.concatenate(v)
        params = jnp.concatenate([norm_gains, norm_biases]).reshape(1, 8 * feats)
        params = jnp.pad(params, ((0, 7), (0, 2 * self_out.shape[1] - 8 * feats)))
        ffn = lax.all_gather(
            ffn_proj, "dp", axis=1, tiled=True, axis_index_groups=[plane_first]
        )
        if direct:
            up, down = placed_weights(place, ffn)
        else:
            up, down = [mm(replace, ffn[i]).astype(BF) for i in (0, 1)]
            place = jnp.zeros((1,), jnp.int32)
        s_a = above(beside(self_qkv[0], self_qkv[1]), beside(self_qkv[2], self_out), params)
        s_c = above(beside(cross_qkv[1], cross_qkv[2]), beside(cross_qkv[0], cross_out))
        held_a, token = gather_far(s_a, far, norm_gains)
        sides_a = gather_sides(held_a, token)
        held_c, token = gather_far(s_c, far, token)
        corner_a = gather_corner(*sides_a, feats, sides_a)
        sides_c = gather_sides(held_c, sides_a)
        corner_c = gather_corner(*sides_c, feats, sides_c)
        weights = [
            gathered(held_a, sides_a, corner_a, feats),
            gathered(held_c, sides_c, corner_c, feats),
        ]
        w_qk, w_vo = full_weight(weights[0], 0, feats), full_weight(weights[0], feats, 2 * feats)
        params = weights[0](2 * feats, 2 * feats + 8)[:, 0, : 8 * feats]
        params = params.reshape(n_dp, 8, feats).transpose(1, 0, 2).reshape(8, width).astype(F32)
        c_kv, c_qo = [full_weight(weights[1], i * feats, (i + 1) * feats) for i in (0, 1)]
        inner_cols = self_out.shape[1]
        w_v, w_o = w_vo[:, :inner_cols], w_vo[:, inner_cols:]
        c_q, c_o = c_qo[:, :inner_cols], c_qo[:, inner_cols:]

        def whole(mine):
            other = swap(mine)
            return jnp.where(
                core == 0,
                jnp.concatenate([mine, other]),
                jnp.concatenate([other, mine]),
            )

        def relabeled(values):
            return mm(values, relabel).astype(BF)

        def own(values):
            size = values.shape[0] // 2
            return lax.dynamic_slice_in_dim(values, core * size, size)

        def other(values):
            size = values.shape[0] // 2
            return lax.dynamic_slice_in_dim(values, (1 - core) * size, size)

        def restored(values):
            high = values.astype(BF)
            low = (values - high.astype(F32)).astype(BF)
            return mm_t(high, relabel) + mm_t(low, relabel)

        x0 = whole(relabeled(tokens))
        enc = whole(relabeled(enc_states))
        cot = whole(relabeled(cotangent))

        hat0, rstd0 = normalize(x0.astype(F32))
        normed1 = (hat0 * params[0] + params[4]).astype(BF)
        qk1 = mm(normed1, w_qk).astype(BF)
        v1 = mm(normed1, w_v).astype(BF)
        first = (qk1, 0), (qk1, inner_cols), (v1, 0)
        o1, logs1 = attend(utt_lengths, *first, inner_cols, True)
        y1 = mm_t(o1, w_o).astype(BF)
        x1, normed2 = norm_rows(1, x0, y1, swap(y1), params)
        kv2 = mm(enc, c_kv).astype(BF)
        q2 = mm(normed2, c_q).astype(BF)
        second = (q2, 0), (kv2, 0), (kv2, inner_cols)
        q2, up, down = lax.optimization_barrier((q2, up, down))
        second = (q2, 0), (kv2, 0), (kv2, inner_cols)
        o2, logs2 = attend(enc_lengths, *second, inner_cols, False)
        y2 = mm_t(o2, c_o).astype(BF)
        x2, normed3 = norm_rows(2, x1, y2, swap(y2), params)
        act, slope = gelu_both(mm(normed3, up))
        act, slope = lax.optimization_barrier((act.astype(BF), slope.astype(BF)))
        y3 = mm_t(act, down).astype(BF)
        out, dx3, dy3, sums3 = norm_last(utt_lengths, x2, y3, swap(y3), params, cot)

        def for_planes(x, d):
            full = outer(place, x, d)
            return full if direct else t_mm(replace, full).astype(BF)

        d_down = for_planes(dy3, act)
        s_down = sum_plane(d_down)
        du = (mm(behind(dy3, d_down), down) * slope.astype(F32)).astype(BF)
        n3 = mm_t(du, up).astype(BF)
        s_up = sum_plane(for_planes(normed3, du))
        dx2, dy2, sums2 = norm_rows_back(2, x2, n3, swap(n3), dx3, params)
        do2 = mm(dy2, c_o).astype(BF)
        dq2, dk2, dv2 = attend_back(
            enc_lengths, *second, do2, logs2, inner_cols, False
        )
        terms_c = grad_terms((enc, normed2, dy2), (0, 0, 1, 2), (dk2, dv2, dq2, o2))
        n2 = mm_t(dq2, c_q).astype(BF)
        dx1, dy1, sums1 = norm_rows_back(1, x1, n2, swap(n2), dx2, params)
        do1 = mm(dy1, w_o).astype(BF)
        dq1, dk1, dv1 = attend_back(
            utt_lengths, *first, do1, logs1, inner_cols, True
        )
        own_c, sent_c, got_c = scatter_near(terms_c, do1)
        terms_qk = grad_terms((normed1,), (0, 0), (dq1, dk1))
        terms_vo = grad_terms((normed1, dy1), (0, 1), (dv1, o1), True)
        n1 = (mm_t(beside(dq1, dk1), w_qk) + mm_t(dv1, w_v)).astype(BF)
        dx0, sums0 = norm_rows_back(0, x0, n1, swap(n1), dx1, params)
        token_grad = restored(own(dx0))
        output = mm_t(own(out), relabel).astype(BF)
        enc_part = mm_t(dk2, c_kv[:, :inner_cols]) + mm_t(dv2, c_kv[:, inner_cols:])
        enc_grad = restored(own(enc_part) + swap(other(enc_part).astype(BF)).astype(F32))

        s_down = line_hops(s_down)
        own_qk, sent_qk, got_qk = scatter_near(terms_qk, dx0)
        s_up = sum_lines(behind(s_up, sent_qk))
        s_cross = scatter_far(near_total(own_c, got_c).astype(BF))
        s_vo, sent_vo, got_vo = scatter_near(lines_first(*terms_vo), sent_qk)
        s_vo = near_total(s_vo, got_vo)
        s_qk = scatter_far(near_total(own_qk, got_qk).astype(BF))
        sums = (sums0, sums1, sums2, sums3)
        terms = jnp.concatenate([v[:1] for v in sums] + [v[1:] for v in sums])
        terms = scatter_small(terms, got_qk)
        part = terms.shape[1] // 2
        terms = lax.dynamic_slice_in_dim(terms, core * part, part, axis=1)
        return (
            output,
            token_grad,
            enc_grad,
            jnp.concatenate([s_qk, s_vo[:1]]),
            s_vo[1],
            jnp.concatenate([s_cross[2:3], s_cross[:2]]),
            s_cross[3],
            jnp.stack([s_up.astype(F32), s_down]),
            terms[:4],
            terms[4:],
        )

    return body


def solution(mesh):
    return jax.shard_map(
        make_body(mesh.shape["dp"]),
        mesh=mesh,
        in_specs=(
            P(("dp", "tensor"), None),
            P(("dp", "tensor"), None),
            P("dp"),
            P("dp"),
            P(None, "dp", "tensor"),
            P("dp", "tensor"),
            P(None, "dp", "tensor"),
            P("dp", "tensor"),
            P(None, "dp", "tensor"),
            P(None, "dp"),
            P(None, "dp"),
            P(("dp", "tensor"), None),
        ),
        out_specs=(
            P(("dp", "tensor"), None),
            P(("dp", "tensor"), None),
            P(("dp", "tensor"), None),
            P(None, "dp", "tensor"),
            P("dp", "tensor"),
            P(None, "dp", "tensor"),
            P("dp", "tensor"),
            P(None, "dp", "tensor"),
            P(None, ("dp", "tensor")),
            P(None, ("dp", "tensor")),
        ),
        check_vma=False,
    )
```

```python
import functools

import jax
import jax.numpy as jnp
from jax import lax
from jax.experimental import pallas as pl
from jax.experimental.pallas import tpu as pltpu
from jax.sharding import PartitionSpec as P

HEAD_DIM = 64
EPSILON = 1e-05
NEG_FILL = -1000000000.0
BF = jnp.bfloat16
F32 = jnp.float32


def dot(a, b, dims):
    return lax.dot_general(a, b, (dims, ((), ())), preferred_element_type=F32)


def mm(a, b):
    return dot(a, b, ((1,), (0,)))


def mm_t(a, b):
    return dot(a, b, ((1,), (1,)))


def t_mm(a, b):
    return dot(a, b, ((0,), (0,)))


def swap(values):
    return lax.ppermute(values, "tensor", [(0, 1), (1, 0)])


def normalize(values):
    centre = jnp.mean(values, axis=-1, keepdims=True)
    centred = values - centre
    spread = jnp.mean(centred * centred, axis=-1, keepdims=True)
    rstd = lax.rsqrt(spread + EPSILON)
    return centred * rstd, rstd


def gelu_both(z):
    c = 0.7978845608028654
    square = z * z
    t = jnp.tanh(z * (c + 0.044715 * c * square))
    gate = 0.5 + 0.5 * t
    value = z * gate
    return value, gate + value * (1.0 - t) * (c + 3.0 * 0.044715 * c * square)


def masked(values, head):
    lane = lax.broadcasted_iota(jnp.int32, values.shape, 1)
    return jnp.where((lane < HEAD_DIM) == (head == 0), values, jnp.zeros_like(values))


def scores_of(keys, queries, start, limit, causal):
    raw = mm_t(keys, queries)
    key = lax.broadcasted_iota(jnp.int32, raw.shape, 0)
    allowed = key < limit
    if causal:
        query = start + lax.broadcasted_iota(jnp.int32, raw.shape, 1)
        allowed = allowed & (key <= query)
    return jnp.where(allowed, raw, NEG_FILL)


def blocks_of(rows, count, causal):
    if causal:
        half = rows // 2
        return [(0, half, half), (half, half, count)]
    return [(0, rows, count)]


def forward_kernel(causal, limit_ref, q_ref, k_ref, v_ref, out_ref, log_ref):
    limit = limit_ref[0]
    scale = HEAD_DIM ** (-0.5)
    for start, size, reach in blocks_of(q_ref.shape[0], k_ref.shape[0], causal):
        queries = (q_ref[start : start + size, :].astype(F32) * scale).astype(BF)
        mixed = None
        for head in range(2):
            keys = masked(k_ref[:reach, :], head)
            values = masked(v_ref[:reach, :], head)
            scores = scores_of(keys, queries, start, limit, causal)
            top = jnp.max(scores, axis=0, keepdims=True)
            exps = jnp.exp(scores - top)
            total = jnp.sum(exps, axis=0, keepdims=True)
            probs = (exps * (1.0 / total)).astype(BF)
            part = t_mm(probs, values)
            mixed = part if mixed is None else mixed + part
            log_ref[0, head : head + 1, start : start + size] = top + jnp.log(total)
        out_ref[start : start + size, :] = mixed.astype(BF)


def backward_kernel(
    causal, limit_ref, q_ref, k_ref, v_ref, do_ref, log_ref, dq_ref, dk_ref, dv_ref, sk, sv
):
    limit = limit_ref[0]
    scale = HEAD_DIM ** (-0.5)
    sk[...] = jnp.zeros_like(sk)
    sv[...] = jnp.zeros_like(sv)
    for start, size, reach in blocks_of(q_ref.shape[0], k_ref.shape[0], causal):
        queries = (q_ref[start : start + size, :].astype(F32) * scale).astype(BF)
        grad = do_ref[start : start + size, :]
        total = None
        for head in range(2):
            keys = masked(k_ref[:reach, :], head)
            values = masked(v_ref[:reach, :], head)
            scores = scores_of(keys, queries, start, limit, causal)
            probs = jnp.exp(scores - log_ref[0, head : head + 1, start : start + size])
            sv[:reach, :] += mm(probs.astype(BF), masked(grad, head))
            dprobs = mm_t(values, grad)
            inner = jnp.sum(dprobs * probs, axis=0, keepdims=True)
            ds = (probs * (dprobs - inner)).astype(BF)
            sk[:reach, :] += mm(ds, masked(queries, head))
            part = t_mm(ds, keys)
            total = part if total is None else total + part
        dq_ref[start : start + size, :] = (total * scale).astype(BF)
    dk_ref[...] = sk[...].astype(BF)
    dv_ref[...] = sv[...].astype(BF)


VMEM_LIMIT = 16 * 1024 * 1024


def params_of():
    return pltpu.CompilerParams(
        dimension_semantics=("arbitrary",), vmem_limit_bytes=VMEM_LIMIT
    )


def column_spec(rows, offset):
    return pl.BlockSpec((rows, 2 * HEAD_DIM), lambda i: (0, i + offset))


def log_spec(rows):
    return pl.BlockSpec((1, 2, rows), lambda i: (i, 0, 0))


SCALAR = pl.BlockSpec(memory_space=pltpu.SMEM)


def attend(limit, q, k, v, cols, causal):
    pairs = cols // (2 * HEAD_DIM)
    rows, count = q[0].shape[0], k[0].shape[0]
    work = rows * count * cols
    return pl.pallas_call(
        functools.partial(forward_kernel, causal),
        grid=(pairs,),
        in_specs=[SCALAR]
        + [column_spec(a.shape[0], at * pairs // cols) for a, at in (q, k, v)],
        out_specs=[column_spec(rows, 0), log_spec(rows)],
        out_shape=[
            jax.ShapeDtypeStruct((rows, cols), BF),
            jax.ShapeDtypeStruct((pairs, 2, rows), F32),
        ],
        compiler_params=params_of(),
        cost_estimate=pl.CostEstimate(
            flops=4 * work, bytes_accessed=8 * rows * cols, transcendentals=work // HEAD_DIM
        ),
    )(limit, q[0], k[0], v[0])


def attend_back(limit, q, k, v, grad, logs, cols, causal):
    pairs = cols // (2 * HEAD_DIM)
    rows, count = q[0].shape[0], k[0].shape[0]
    work = rows * count * cols
    return pl.pallas_call(
        functools.partial(backward_kernel, causal),
        grid=(pairs,),
        in_specs=[SCALAR]
        + [column_spec(a.shape[0], at * pairs // cols) for a, at in (q, k, v)]
        + [column_spec(rows, 0), log_spec(rows)],
        out_specs=[column_spec(rows, 0), column_spec(count, 0), column_spec(count, 0)],
        out_shape=[jax.ShapeDtypeStruct((n, cols), BF) for n in (rows, count, count)],
        scratch_shapes=[pltpu.VMEM((count, 2 * HEAD_DIM), F32) for i in range(2)],
        compiler_params=params_of(),
        cost_estimate=pl.CostEstimate(
            flops=10 * work, bytes_accessed=16 * rows * cols, transcendentals=work // HEAD_DIM
        ),
    )(limit, q[0], k[0], v[0], grad, logs)


def row_spec(rows, cols):
    return pl.BlockSpec((rows, cols), lambda i: (i, 0))


def fixed_spec(*shape):
    return pl.BlockSpec(shape, lambda i: (0,) * len(shape))


CHUNK = 16


def fold(values):
    return values[: CHUNK // 2] + values[CHUNK // 2 :]


def chunked(step, visit, width, sum_ref=None):
    zero = jnp.zeros((CHUNK // 2, width), F32)
    gain, shift = zero, zero
    for start in range(0, step, CHUNK):
        terms = visit(slice(start, start + CHUNK))
        if sum_ref is not None:
            gain, shift = gain + fold(terms[0]), shift + fold(terms[1])
    if sum_ref is None:
        return
    sums = jnp.concatenate(
        [jnp.sum(gain, axis=0, keepdims=True), jnp.sum(shift, axis=0, keepdims=True)]
    )
    first = pl.program_id(0) == 0

    @pl.when(first)
    def _():
        sum_ref[...] = sums

    @pl.when(jnp.logical_not(first))
    def _():
        sum_ref[...] += sums


def norm_grad(hat, rstd, gain, grad):
    scaled = grad * gain
    first = jnp.mean(scaled, axis=-1, keepdims=True)
    second = jnp.mean(scaled * hat, axis=-1, keepdims=True)
    return rstd * (scaled - first - hat * second)


def norm_kernel(index, x_ref, own_ref, other_ref, p_ref, new_ref, out_ref):
    step, width = x_ref.shape
    gain, shift = p_ref[index : index + 1, :], p_ref[index + 4 : index + 5, :]

    def visit(at):
        x = x_ref[at, :].astype(F32) + own_ref[at, :].astype(F32) + other_ref[at, :].astype(F32)
        new_ref[at, :] = x
        hat, rstd = normalize(x)
        out_ref[at, :] = (hat * gain + shift).astype(BF)

    chunked(step, visit, width)


def norm_rows(index, x, own, other, params):
    rows, width = x.shape
    step = rows // 2
    row = row_spec(step, width)
    return pl.pallas_call(
        functools.partial(norm_kernel, index),
        grid=(2,),
        in_specs=[row, row, row, fixed_spec(*params.shape)],
        out_specs=[row, row],
        out_shape=[
            jax.ShapeDtypeStruct((rows, width), F32),
            jax.ShapeDtypeStruct((rows, width), BF),
        ],
        compiler_params=params_of(),
        cost_estimate=pl.CostEstimate(
            flops=20 * rows * width, bytes_accessed=14 * rows * width, transcendentals=rows
        ),
    )(x, own, other, params)


def last_kernel(
    limit_ref, x_ref, own_ref, other_ref, p_ref, cot_ref, out_ref, dx_ref, dy_ref, sum_ref
):
    step, width = x_ref.shape
    gain, shift = p_ref[3:4, :], p_ref[7:8, :]
    begin = pl.program_id(0) * step

    def visit(at):
        x = x_ref[at, :] + own_ref[at, :].astype(F32) + other_ref[at, :].astype(F32)
        hat, rstd = normalize(x)
        out_ref[at, :] = (hat * gain + shift).astype(BF)
        row = begin + at.start + lax.broadcasted_iota(jnp.int32, (CHUNK, 1), 0)
        grad = cot_ref[at, :].astype(F32) * (row < limit_ref[0]).astype(F32)
        dx = norm_grad(hat, rstd, gain, grad)
        dx_ref[at, :] = dx
        dy_ref[at, :] = dx.astype(BF)
        return grad * hat, grad

    chunked(step, visit, width, sum_ref)


def norm_last(limit, x, own, other, params, cot):
    rows, width = x.shape
    step = rows // 2
    row = row_spec(step, width)
    return pl.pallas_call(
        last_kernel,
        grid=(2,),
        in_specs=[SCALAR, row, row, row, fixed_spec(*params.shape), row],
        out_specs=[row, row, row, fixed_spec(2, width)],
        out_shape=[
            jax.ShapeDtypeStruct((rows, width), BF),
            jax.ShapeDtypeStruct((rows, width), F32),
            jax.ShapeDtypeStruct((rows, width), BF),
            jax.ShapeDtypeStruct((2, width), F32),
        ],
        compiler_params=params_of(),
        cost_estimate=pl.CostEstimate(
            flops=40 * rows * width, bytes_accessed=20 * rows * width, transcendentals=rows
        ),
    )(limit, x, own, other, params, cot)


def back_kernel(index, x_ref, own_ref, other_ref, dres_ref, p_ref, dx_ref, *refs):
    step, width = x_ref.shape
    gain = p_ref[index : index + 1, :]

    def visit(at):
        hat, rstd = normalize(x_ref[at, :].astype(F32))
        grad = own_ref[at, :].astype(F32) + other_ref[at, :].astype(F32)
        dx = dres_ref[at, :] + norm_grad(hat, rstd, gain, grad)
        dx_ref[at, :] = dx
        if index:
            refs[0][at, :] = dx.astype(BF)
        return grad * hat, grad

    chunked(step, visit, width, refs[-1])


def norm_rows_back(index, x, own, other, dres, params):
    rows, width = x.shape
    step = rows // 2
    row = row_spec(step, width)
    lower = 1 if index else 0
    return pl.pallas_call(
        functools.partial(back_kernel, index),
        grid=(2,),
        in_specs=[row, row, row, row, fixed_spec(*params.shape)],
        out_specs=[row] + [row] * lower + [fixed_spec(2, width)],
        out_shape=[jax.ShapeDtypeStruct((rows, width), F32)]
        + [jax.ShapeDtypeStruct((rows, width), BF)] * lower
        + [jax.ShapeDtypeStruct((2, width), F32)],
        compiler_params=params_of(),
        cost_estimate=pl.CostEstimate(
            flops=30 * rows * width, bytes_accessed=18 * rows * width, transcendentals=rows
        ),
    )(x, own, other, dres, params)


FFN_STEPS = 4


def place_kernel(place_ref, from_ref, up_ref, down_ref, sems):
    blocks = place_ref.shape[0]
    size = up_ref.shape[0] // blocks
    copies = []
    for half, to_ref in enumerate((up_ref, down_ref)):
        for label in range(blocks):
            at = pl.multiple_of(place_ref[label] * size, size)
            copy = pltpu.make_async_copy(
                from_ref.at[half, pl.ds(at, size), :],
                to_ref.at[pl.ds(label * size, size), :],
                sems.at[half, label],
            )
            copy.start()
            copies.append(copy)
    for copy in copies:
        copy.wait()


def placed_weights(place, ffn):
    parts, width, units = ffn.shape
    anywhere = pl.BlockSpec(memory_space=pl.ANY)
    return pl.pallas_call(
        place_kernel,
        in_specs=[SCALAR, pl.BlockSpec(memory_space=pltpu.HBM)],
        out_specs=[anywhere] * 2,
        out_shape=[jax.ShapeDtypeStruct((width, units), BF)] * 2,
        scratch_shapes=[pltpu.SemaphoreType.DMA((2, place.shape[0]))],
        compiler_params=pltpu.CompilerParams(vmem_limit_bytes=1024 * 1024),
        cost_estimate=pl.CostEstimate(
            flops=0, bytes_accessed=4 * parts * width * units, transcendentals=0
        ),
    )(place, ffn)


def outer_kernel(place_ref, x_ref, d_ref, out_ref, turned):
    @pl.when(pl.program_id(0) == 0)
    def _():
        turned[...] = x_ref[...].T

    full = mm(turned[...], d_ref[...]).astype(BF)
    blocks = place_ref.shape[0]
    size = full.shape[0] // blocks
    for label in range(blocks):
        at = pl.multiple_of(place_ref[label] * size, size)
        out_ref[pl.ds(at, size), :] = full[label * size : (label + 1) * size]


def outer(place, x, d):
    rows, width = x.shape
    units = d.shape[1]
    step = units // FFN_STEPS
    col = pl.BlockSpec((width, step), lambda i: (0, i))
    return pl.pallas_call(
        outer_kernel,
        grid=(FFN_STEPS,),
        in_specs=[SCALAR, fixed_spec(rows, width), pl.BlockSpec((rows, step), lambda i: (0, i))],
        out_specs=col,
        out_shape=pltpu.HBM((width, units), BF),
        scratch_shapes=[pltpu.VMEM((width, rows), BF)],
        compiler_params=params_of(),
        cost_estimate=pl.CostEstimate(
            flops=2 * rows * width * units,
            bytes_accessed=2 * width * units + 2 * rows * units,
            transcendentals=0,
        ),
    )(place, x, d)


def terms_kernel(order, lines, *refs):
    step = pl.program_id(0)
    count, blocks = len(set(order)), len(order)
    lefts, rights, refs = refs[:count], refs[count : count + blocks], refs[count + blocks :]
    turned = refs[-count:]
    for block in range(blocks):

        @pl.when(step == block)
        def _(block=block):
            at = order[block]
            if order.index(at) == block:
                turned[at][...] = lefts[at][...].T
            full = mm(turned[at][...], rights[block][...]).astype(BF)
            quarter = full.shape[0] // 4
            if lines:
                keep_ref, send_ref = refs[:2]
                half = quarter // 2
                for label in range(4):
                    middle = label * quarter + half
                    keep_ref[0, label] = full[middle - half : middle]
                    send_ref[0, label] = full[middle : middle + half]
            else:
                one_ref, two_ref, y_ref, x_ref, own_ref = refs[:5]
                own_ref[0] = full[:quarter]
                y_ref[0] = full[quarter : 2 * quarter]
                x_ref[0] = full[2 * quarter : 3 * quarter]
                (one_ref if block < blocks // 2 else two_ref)[0] = full[3 * quarter :]


def grad_terms(lefts, order, rights, lines=False):
    width, cols = lefts[0].shape[1], rights[0].shape[1]
    blocks = len(order)
    middle = blocks // 2
    quarter = width // 4
    same = lambda i: i
    if lines:
        spec = pl.BlockSpec((1, 4, quarter // 2, cols), lambda i: (i, 0, 0, 0))
        out_specs = [spec] * 2
        out_shape = [jax.ShapeDtypeStruct((blocks, 4, quarter // 2, cols), BF)] * 2
    else:
        piece = lambda place: pl.BlockSpec((1, quarter, cols), lambda i: (place(i), 0, 0))
        shape = lambda n: jax.ShapeDtypeStruct((n, quarter, cols), BF)
        out_specs = [
            piece(lambda i: jnp.minimum(i, middle - 1)),
            piece(lambda i: jnp.maximum(i - middle, 0)),
        ] + [piece(same)] * 3
        out_shape = [shape(middle)] * 2 + [shape(blocks)] * 3
    return pl.pallas_call(
        functools.partial(terms_kernel, order, lines),
        grid=(blocks,),
        in_specs=[fixed_spec(*v.shape) for v in (*lefts, *rights)],
        out_specs=out_specs,
        out_shape=out_shape,
        scratch_shapes=[pltpu.VMEM((width, v.shape[0]), BF) for v in lefts],
        compiler_params=params_of(),
        cost_estimate=pl.CostEstimate(
            flops=2 * blocks * lefts[0].shape[0] * width * cols,
            bytes_accessed=2 * blocks * width * cols + 16 * lefts[0].shape[0] * width,
            transcendentals=0,
        ),
    )(*lefts, *rights)


def behind(values, earlier):
    return lax.optimization_barrier((values, earlier))[0]


def make_body(n_dp):
    bits = n_dp.bit_length() - 1
    assert n_dp == 1 << bits

    def hop(values, bit):
        return lax.ppermute(values, "dp", [(i, i ^ (1 << bit)) for i in range(n_dp)])

    far = range(bits - 1, 1, -1)

    def gather_far(held, bits_now, after):
        for bit in bits_now:
            after = hop(behind(held, after), bit)
            held = jnp.stack([held, after])
        return held, after

    def inner_rows(v, start, stop):
        return lax.slice_in_dim(v, start, stop, axis=v.ndim - 2)

    def gather_sides(held, after):
        held = behind(held, after)
        return hop(held, 0), hop(held, 1)

    def gather_corner(by_x, by_y, cut, after):
        first = behind(inner_rows(by_y, 0, cut), after)
        second = behind(inner_rows(by_x, cut, by_x.shape[-2]), after)
        return hop(first, 0), hop(second, 1)

    def gathered(held, sides, corner, cut):
        (by_x, by_y), (first, second) = sides, corner

        def rows(start, stop):
            last, offset = (first, 0) if stop <= cut else (second, cut)
            parts = [inner_rows(v, start, stop) for v in (held, by_y, by_x)]
            parts.append(inner_rows(last, start - offset, stop - offset))
            return jnp.concatenate(
                [v.reshape(-1, stop - start, v.shape[-1]) for v in parts]
            )

        return rows

    def full_weight(rows, start, stop):
        return rows(start, stop).reshape(-1, rows(start, stop).shape[-1])

    def plus(v, w):
        return (v.astype(F32) + w.astype(F32)).astype(BF)

    def scatter_near(pieces, late):
        one, two, for_y, for_x, own = pieces
        middle = one.shape[0]
        got_one, got_two = behind((hop(one, 0), hop(two, 1)), late)
        for_y = for_y.at[:middle].set(plus(for_y[:middle], got_one))
        for_x = for_x.at[middle:].set(plus(for_x[middle:], got_two))
        got_x, got_y = hop(for_x, 0), hop(for_y, 1)
        return own, (for_x, for_y), (got_x, got_y)

    def near_total(own, got):
        return own.astype(F32) + got[0].astype(F32) + got[1].astype(F32)

    def scatter_far(held):
        parts, feats, cols = held.shape
        held = held.reshape(parts, -1, feats * 4 // n_dp, cols)
        for count, bit in enumerate(reversed(far)):
            middle = held.shape[1] // 2
            held = held[:, :middle].astype(F32) + hop(held[:, middle:], bit).astype(F32)
            if count < len(far) - 1:
                held = held.astype(BF)
        return held[:, 0]

    def lines_first(keep, send):
        for count, bit in enumerate(reversed(far)):
            if count:
                middle = keep.shape[2] // 2
                keep, send = keep[:, :, :middle], keep[:, :, middle:]
            keep = plus(keep, hop(send, bit))
        middle = keep.shape[0] // 2
        return keep[:middle, 3], keep[middle:, 3], keep[:, 1], keep[:, 2], keep[:, 0]

    planes = [[4 * z + p for p in range(4)] for z in range(n_dp // 4)]
    lines = [[4 * z + p for z in range(n_dp // 4)] for p in range(4)]
    plane_first = [chip for line in lines for chip in line]

    def sum_plane(full):
        return lax.psum_scatter(
            full, "dp", scatter_dimension=0, tiled=True, axis_index_groups=planes
        )

    def sum_lines(full):
        return lax.psum_scatter(
            full, "dp", scatter_dimension=0, tiled=True, axis_index_groups=lines
        )

    def line_hops(full):
        rows, cols = full.shape
        held = full.reshape((2,) * len(far) + (rows * 4 // n_dp, cols))
        for count, bit in enumerate(reversed(far)):
            mine = (lax.axis_index("dp") >> bit) & 1
            axis = held.ndim - 3
            keep = lax.dynamic_index_in_dim(held, mine, axis, keepdims=False)
            send = lax.dynamic_index_in_dim(held, 1 - mine, axis, keepdims=False)
            held = keep.astype(F32) + hop(send.astype(BF), bit).astype(F32)
        return held

    def scatter_small(full, late):
        lead, feats = full.shape
        held = full.reshape((lead,) + (2,) * bits + (feats // n_dp,))
        for bit in reversed(far):
            keep = lax.index_in_dim(held, 0, 3, keepdims=False)
            held = keep + hop(lax.index_in_dim(held, 1, 3, keepdims=False), bit)
        held = behind(held, late)
        for bit in (0, 1):
            keep = lax.index_in_dim(held, 0, 1, keepdims=False)
            held = keep + hop(lax.index_in_dim(held, 1, 1, keepdims=False), bit)
        return held

    def body(
        tokens,
        enc_states,
        utt_lengths,
        enc_lengths,
        self_qkv,
        self_out,
        cross_qkv,
        cross_out,
        ffn_proj,
        norm_gains,
        norm_biases,
        cotangent,
    ):
        width = tokens.shape[1]
        feats = norm_gains.shape[1]
        core = lax.axis_index("tensor")
        me = lax.axis_index("dp")

        block = width // n_dp
        cols = jnp.arange(width, dtype=jnp.int32)
        labels = cols // block
        reverse = jnp.zeros_like(labels)
        for bit in range(bits):
            reverse = reverse | (((labels >> (bits - 1 - bit)) & 1) << bit)
        source = (me ^ reverse) * block + cols % block
        relabel = (cols[:, None] == source[None, :]).astype(BF)
        chip = source // block
        placed = ((chip & 3) * (n_dp // 4) + (chip >> 2)) * block + cols % block
        place = placed[::block] // block
        replace = (placed[:, None] == cols[None, :]).astype(BF)
        direct = feats % 16 == 0

        beside = lambda *v: jnp.concatenate(v, axis=-1)
        above = lambda *v: jnp.concatenate(v)
        params = jnp.concatenate([norm_gains, norm_biases]).reshape(1, 8 * feats)
        params = jnp.pad(params, ((0, 7), (0, 2 * self_out.shape[1] - 8 * feats)))
        ffn = lax.all_gather(
            ffn_proj, "dp", axis=1, tiled=True, axis_index_groups=[plane_first]
        )
        if direct:
            up, down = placed_weights(place, ffn)
        else:
            up, down = [mm(replace, ffn[i]).astype(BF) for i in (0, 1)]
            place = jnp.zeros((1,), jnp.int32)
        s_a = above(beside(self_qkv[0], self_qkv[1]), beside(self_qkv[2], self_out), params)
        s_c = above(beside(cross_qkv[1], cross_qkv[2]), beside(cross_qkv[0], cross_out))
        held_a, token = gather_far(s_a, far, norm_gains)
        sides_a = gather_sides(held_a, token)
        held_c, token = gather_far(s_c, far, token)
        corner_a = gather_corner(*sides_a, feats, sides_a)
        sides_c = gather_sides(held_c, sides_a)
        corner_c = gather_corner(*sides_c, feats, sides_c)
        weights = [
            gathered(held_a, sides_a, corner_a, feats),
            gathered(held_c, sides_c, corner_c, feats),
        ]
        w_qk, w_vo = full_weight(weights[0], 0, feats), full_weight(weights[0], feats, 2 * feats)
        params = weights[0](2 * feats, 2 * feats + 8)[:, 0, : 8 * feats]
        params = params.reshape(n_dp, 8, feats).transpose(1, 0, 2).reshape(8, width).astype(F32)
        c_kv, c_qo = [full_weight(weights[1], i * feats, (i + 1) * feats) for i in (0, 1)]
        inner_cols = self_out.shape[1]
        w_v, w_o = w_vo[:, :inner_cols], w_vo[:, inner_cols:]
        c_q, c_o = c_qo[:, :inner_cols], c_qo[:, inner_cols:]

        def whole(mine):
            other = swap(mine)
            return jnp.where(
                core == 0,
                jnp.concatenate([mine, other]),
                jnp.concatenate([other, mine]),
            )

        def relabeled(values):
            return mm(values, relabel).astype(BF)

        def own(values):
            size = values.shape[0] // 2
            return lax.dynamic_slice_in_dim(values, core * size, size)

        def other(values):
            size = values.shape[0] // 2
            return lax.dynamic_slice_in_dim(values, (1 - core) * size, size)

        def restored(values):
            high = values.astype(BF)
            low = (values - high.astype(F32)).astype(BF)
            return mm_t(high, relabel) + mm_t(low, relabel)

        x0 = whole(relabeled(tokens))
        enc = whole(relabeled(enc_states))
        cot = whole(relabeled(cotangent))

        hat0, rstd0 = normalize(x0.astype(F32))
        normed1 = (hat0 * params[0] + params[4]).astype(BF)
        qk1 = mm(normed1, w_qk).astype(BF)
        v1 = mm(normed1, w_v).astype(BF)
        first = (qk1, 0), (qk1, inner_cols), (v1, 0)
        o1, logs1 = attend(utt_lengths, *first, inner_cols, True)
        y1 = mm_t(o1, w_o).astype(BF)
        x1, normed2 = norm_rows(1, x0, y1, swap(y1), params)
        kv2 = mm(enc, c_kv).astype(BF)
        q2 = mm(normed2, c_q).astype(BF)
        second = (q2, 0), (kv2, 0), (kv2, inner_cols)
        q2, up, down = lax.optimization_barrier((q2, up, down))
        second = (q2, 0), (kv2, 0), (kv2, inner_cols)
        o2, logs2 = attend(enc_lengths, *second, inner_cols, False)
        y2 = mm_t(o2, c_o).astype(BF)
        x2, normed3 = norm_rows(2, x1, y2, swap(y2), params)
        act, slope = gelu_both(mm(normed3, up))
        act, slope = lax.optimization_barrier((act.astype(BF), slope.astype(BF)))
        y3 = mm_t(act, down).astype(BF)
        out, dx3, dy3, sums3 = norm_last(utt_lengths, x2, y3, swap(y3), params, cot)

        def for_planes(x, d):
            full = outer(place, x, d)
            return full if direct else t_mm(replace, full).astype(BF)

        d_down = for_planes(dy3, act)
        s_down = sum_plane(d_down)
        du = (mm(behind(dy3, d_down), down) * slope.astype(F32)).astype(BF)
        n3 = mm_t(du, up).astype(BF)
        s_up = sum_plane(for_planes(normed3, du))
        dx2, dy2, sums2 = norm_rows_back(2, x2, n3, swap(n3), dx3, params)
        do2 = mm(dy2, c_o).astype(BF)
        dq2, dk2, dv2 = attend_back(
            enc_lengths, *second, do2, logs2, inner_cols, False
        )
        terms_c = grad_terms((enc, normed2, dy2), (0, 0, 1, 2), (dk2, dv2, dq2, o2))
        n2 = mm_t(dq2, c_q).astype(BF)
        dx1, dy1, sums1 = norm_rows_back(1, x1, n2, swap(n2), dx2, params)
        do1 = mm(dy1, w_o).astype(BF)
        dq1, dk1, dv1 = attend_back(
            utt_lengths, *first, do1, logs1, inner_cols, True
        )
        own_c, sent_c, got_c = scatter_near(terms_c, do1)
        terms_qk = grad_terms((normed1,), (0, 0), (dq1, dk1))
        terms_vo = grad_terms((normed1, dy1), (0, 1), (dv1, o1), True)
        n1 = (mm_t(beside(dq1, dk1), w_qk) + mm_t(dv1, w_v)).astype(BF)
        dx0, sums0 = norm_rows_back(0, x0, n1, swap(n1), dx1, params)
        token_grad = restored(own(dx0))
        output = mm_t(own(out), relabel).astype(BF)
        enc_part = mm_t(dk2, c_kv[:, :inner_cols]) + mm_t(dv2, c_kv[:, inner_cols:])
        enc_grad = restored(own(enc_part) + swap(other(enc_part).astype(BF)).astype(F32))

        s_down = line_hops(s_down)
        own_qk, sent_qk, got_qk = scatter_near(terms_qk, dx0)
        s_up = sum_lines(behind(s_up, sent_qk))
        s_cross = scatter_far(near_total(own_c, got_c).astype(BF))
        s_vo, sent_vo, got_vo = scatter_near(lines_first(*terms_vo), sent_qk)
        s_vo = near_total(s_vo, got_vo)
        s_qk = scatter_far(near_total(own_qk, got_qk).astype(BF))
        sums = (sums0, sums1, sums2, sums3)
        terms = jnp.concatenate([v[:1] for v in sums] + [v[1:] for v in sums])
        terms = scatter_small(terms, got_qk)
        part = terms.shape[1] // 2
        terms = lax.dynamic_slice_in_dim(terms, core * part, part, axis=1)
        return (
            output,
            token_grad,
            enc_grad,
            jnp.concatenate([s_qk, s_vo[:1]]),
            s_vo[1],
            jnp.concatenate([s_cross[2:3], s_cross[:2]]),
            s_cross[3],
            jnp.stack([s_up.astype(F32), s_down]),
            terms[:4],
            terms[4:],
        )

    return body


def solution(mesh):
    return jax.shard_map(
        make_body(mesh.shape["dp"]),
        mesh=mesh,
        in_specs=(
            P(("dp", "tensor"), None),
            P(("dp", "tensor"), None),
            P("dp"),
            P("dp"),
            P(None, "dp", "tensor"),
            P("dp", "tensor"),
            P(None, "dp", "tensor"),
            P("dp", "tensor"),
            P(None, "dp", "tensor"),
            P(None, "dp"),
            P(None, "dp"),
            P(("dp", "tensor"), None),
        ),
        out_specs=(
            P(("dp", "tensor"), None),
            P(("dp", "tensor"), None),
            P(("dp", "tensor"), None),
            P(None, "dp", "tensor"),
            P("dp", "tensor"),
            P(None, "dp", "tensor"),
            P("dp", "tensor"),
            P(None, "dp", "tensor"),
            P(None, ("dp", "tensor")),
            P(None, ("dp", "tensor")),
        ),
        check_vma=False,
    )
```
